128 devices in a mesh: gz: 2 (over core), xy: 64 (over y, z, x).
Axes of the slice: x: 4, y: 4, z: 4, core: 2. Of those that a mesh axis runs over, the one named last changes fastest.
Arguments:
- image: bfloat16 [2, 64, 4, 1, 128, 512], P('gz', 'xy'), may hold values from -6 to 6
- bricks: bfloat16 [2, 64, 4, 1, 128, 1000], P('gz', 'xy'), may hold values from -6 to 6
- owner: int32 [2, 64, 4, 1, 128, 1], P('gz', 'xy'), may hold values from 0 to 127; in each aligned block of 512 rows (0 to 511, 512 to 1023, ..., all dimensions but the last counted through in order) at most 16 rows name the same one
- brick_index: int32 [2, 64, 4, 1, 128], P('gz', 'xy'), may hold values from 0 to 511
- offset_class: int32 [2, 64, 4, 1, 128], P('gz', 'xy'), may hold values from 0 to 63
Outputs:
- nodes: float32 [9, 8, 64, 128], P(None, 'gz', 'xy')
- gram: float32 [2, 64, 4, 1, 128, 576], P('gz', 'xy')
The draws below stay inside these ranges and needn't reach their ends.
Inputs may be any that keep to these rules, and one draw needn't show every extreme that they name: At most 16 elements of one device take bricks from one owner, and in some device's block one owner is named by exactly 16 elements.
All inputs are finite; a program needn't handle non-finite values.
Results may differ from the reference program's by a relative error of at most 0.0025.
Values may be sent and summed in bfloat16 or wider, within the bound.
A program may use at most 128 MiB of HBM per device.

```python
import math
import jax
import jax.numpy as jnp
import numpy as np
from jax import lax

EZ = 4
EX = 1
EY = 128
E_DEV = 512
CAP = 16
NZE = 8
NXE = 64
N_GZ = 2
N_XY = 64
DEVICES = 128


def set_ends(drawn, rng, least, top_value):
    dims = drawn.shape
    spot = [jax.random.randint(jax.random.fold_in(rng, axis), (), 0, dims[axis]) for axis in range(len(dims))]
    drawn = drawn.at[tuple(spot)].set(least)
    longest = dims.index(max(dims))
    spot[longest] = (spot[longest] + 1) % dims[longest]
    return drawn.at[tuple(spot)].set(top_value)


def level_of(stream_key, extent, split, smallest, top_value):
    level = 1.0
    for axis_at, blocks in split:
        draws = jax.random.uniform(jax.random.fold_in(jax.random.fold_in(stream_key, 6), axis_at), (blocks,), jnp.float32, smallest / len(split), top_value / len(split))
        level = level * jnp.repeat(jnp.exp(draws), extent[axis_at] // blocks).reshape((-1,) + (1,) * (len(extent) - 1 - axis_at))
    return level


def routed_block(stream_key, own, number, rows, number_of, top, reach, slope):
    ranking = jax.random.permutation(stream_key, number_of)
    packed, common = load_shares(number_of, rows * top, reach, slope, True), load_shares(number_of, rows * top, reach, slope, False)
    places = jnp.arange(number_of)

    def named(sizes, offset_by):
        used = int((sizes > 0).sum())
        fixed = max(1, used // 4)
        shifted = fixed + (places - fixed + offset_by * (used - fixed)) % max(1, number_of - fixed)
        return jnp.zeros((number_of,), jnp.int32).at[ranking[jnp.where(places < fixed, places, shifted)]].set(jnp.asarray(sizes, jnp.int32))

    sizes = jnp.where(number % 4 == 0, named(packed, number // 4), named(common, number - number // 4 - 1))
    mixed = jax.random.permutation(jax.random.fold_in(own, 3), number_of)
    donor, receiver = mixed[0:number_of // 2 * 2:2], mixed[1:number_of // 2 * 2:2]
    slack = jnp.minimum(sizes[donor] - 1, reach - sizes[receiver]) // 2
    slack = jnp.where((donor == ranking[0]) | (receiver == ranking[0]) | (sizes[receiver] == 0), 0, jnp.maximum(slack, 0))
    shifted = jax.random.randint(jax.random.fold_in(own, 4), (number_of // 2,), 0, 1 << 20) % (slack + 1)
    sizes = sizes.at[donor].add(-shifted).at[receiver].add(shifted)
    items = jnp.searchsorted(jnp.cumsum(sizes), jnp.arange(rows * top), side="right").astype(jnp.int32)
    table = items.reshape(top, rows).T
    table = table[jax.random.permutation(jax.random.fold_in(own, 1), rows)]
    offset_by = jax.random.randint(jax.random.fold_in(own, 2), (rows, 1), 0, top)
    return jnp.take_along_axis(table, (jnp.arange(top)[None, :] + offset_by) % top, axis=1)


def load_shares(amount, total, reach, lean, full):
    portions = [(1 << 20) // math.isqrt(grade ** lean) + 1 for grade in range(1, amount + 1)]
    largest = reach if full else min(reach, max(-(-total // amount), total * portions[0] // sum(portions)))
    least = 1 if total - largest >= amount - 1 else 0
    counts, rest = [largest] + [least] * (amount - 1), total - largest - least * (amount - 1)
    while rest > 0:
        movable = [i for i in range(1, amount) if counts[i] < largest] or [i for i in range(1, amount) if counts[i] < reach]
        whole, budget = sum([portions[i] for i in movable]), rest
        for i in movable:
            addition = min(reach - counts[i], max(1, budget * portions[i] // whole), rest)
            counts[i] = counts[i] + addition
            rest = rest - addition
    return np.array(counts)


def scatter_about(key, shape, width, most, cuts=(), kind=jnp.bfloat16):
    result = width * jax.random.normal(key, shape, jnp.float32)
    if cuts:
        result = result * level_of(key, shape, cuts, -0.22, 0.18)
    return jnp.clip(result, -most, most).astype(kind)


def setup_inputs(seed: int = 0) -> dict:
    streams_of = jax.random.split(jax.random.key(seed), 6)
    image = scatter_about(streams_of[0], (N_GZ, N_XY, EZ, EX, EY, 512), 1.0, 6.0, ((0, 2), (1, 64)))
    bricks = scatter_about(streams_of[1], (N_GZ, N_XY, EZ, EX, EY, 1000), 1.0, 6.0, ((0, 2), (1, 64)))
    owner_keys = jax.random.split(jax.random.fold_in(streams_of[2], 1), N_GZ * N_XY * EZ * EX * EY // E_DEV)
    owner_turns = jax.random.permutation(jax.random.fold_in(streams_of[2], 3), N_GZ * N_XY * EZ * EX * EY // E_DEV)
    owner = jax.vmap(lambda own, number: routed_block(jax.random.fold_in(streams_of[2], 2), own, number, E_DEV, DEVICES, 1, CAP, 2))(owner_keys, owner_turns).reshape((N_GZ, N_XY, EZ, EX, EY, 1))
    brick_index = set_ends(jax.random.randint(streams_of[3], (N_GZ, N_XY, EZ, EX, EY), 0, E_DEV), jax.random.fold_in(streams_of[3], 1), 0, E_DEV - 1).astype(jnp.int32)
    offset_class = set_ends(jax.random.randint(streams_of[4], (N_GZ, N_XY, EZ, EX, EY), 0, 64), jax.random.fold_in(streams_of[4], 1), 0, 63).astype(jnp.int32)
    return dict(image=image, bricks=bricks, owner=owner, brick_index=brick_index, offset_class=offset_class)


def corner_fractions(offset):
    frac_z = ((offset // 16).astype(jnp.float32) + 0.5) / 4.0
    frac_x = (((offset // 4) % 4).astype(jnp.float32) + 0.5) / 4.0
    frac_y = ((offset % 4).astype(jnp.float32) + 0.5) / 4.0
    return frac_z, frac_x, frac_y


def deformed_samples(brick_rows, offset):
    cube = brick_rows.astype(jnp.float32).reshape(-1, 10, 10, 10)
    frac_z, frac_x, frac_y = corner_fractions(offset)
    total = jnp.zeros((cube.shape[0], 9, 9, 9), jnp.float32)
    for z_increment in (0, 1):
        weight_z = frac_z if z_increment else 1.0 - frac_z
        for step_x in (0, 1):
            weight_x = frac_x if step_x else 1.0 - frac_x
            for step_y in (0, 1):
                weight_y = frac_y if step_y else 1.0 - frac_y
                weight = (weight_z * weight_x * weight_y)[:, None, None, None]
                total = total + weight * cube[:, z_increment:z_increment + 9, step_x:step_x + 9, step_y:step_y + 9]
    return total.reshape(-1, 729).astype(jnp.bfloat16)


def shape_table():
    centre = (jnp.arange(8, dtype=jnp.float32) + 0.5) / 8.0
    rows = []
    for node_z in (0, 1):
        along_z = centre if node_z else 1.0 - centre
        for node_x in (0, 1):
            x_direction_shape = centre if node_x else 1.0 - centre
            for node_y in (0, 1):
                y_direction_shape = centre if node_y else 1.0 - centre
                rows.append((along_z[:, None, None] * x_direction_shape[None, :, None] * y_direction_shape[None, None, :]).reshape(512))
    return jnp.stack(rows)


def element_terms(samples, image):
    cube = samples.astype(jnp.float32).reshape(-1, 9, 9, 9)
    base = cube[:, :8, :8, :8]
    residual_values = (base - image.astype(jnp.float32).reshape(-1, 8, 8, 8)).reshape(-1, 512)
    slopes = jnp.stack([cube[:, 1:, :8, :8] - base, cube[:, :8, 1:, :8] - base, cube[:, :8, :8, 1:] - base], axis=1)
    slopes = slopes.reshape(-1, 3, 1, 512)
    jacobian_matrix = (slopes * shape_table()[None, None, :, :]).reshape(-1, 24, 512)
    gram = jnp.einsum("hqy,hjy->hqj", jacobian_matrix, jacobian_matrix, precision=lax.Precision.HIGHEST) / 64.0
    residual_vector = jnp.einsum("xeu,xu->xe", jacobian_matrix, residual_values, precision=lax.Precision.HIGHEST) / 64.0
    blocks = jnp.diagonal(gram.reshape(-1, 3, 8, 3, 8), axis1=2, axis2=4)
    pairs = jnp.stack([blocks[:, 0, 0], blocks[:, 0, 1], blocks[:, 0, 2], blocks[:, 1, 1], blocks[:, 1, 2], blocks[:, 2, 2]], axis=1)
    node_terms = jnp.concatenate([residual_vector.reshape(-1, 3, 8), pairs], axis=1)
    return node_terms, gram.reshape(-1, 576)


def reference(image, bricks, owner, brick_index, offset_class):
    count = N_GZ * N_XY * E_DEV
    flat_bricks = bricks.reshape(count, 1000)
    source = (owner.reshape(count) * E_DEV + brick_index.reshape(count)).astype(jnp.int32)
    block = math.gcd(E_DEV, 512)

    def run(items):
        src, cls, img = items
        samples = deformed_samples(jnp.take(flat_bricks, src, axis=0), cls)
        return element_terms(samples, img)

    node_terms, gram = lax.map(run, (source.reshape(-1, block), offset_class.reshape(-1, block), image.reshape(-1, block, 512)))
    terms = node_terms.reshape(N_GZ, N_XY, EZ, EX, EY, 9, 8)
    terms = jnp.transpose(terms, (5, 6, 0, 2, 1, 3, 4)).reshape(9, 8, NZE, NXE, EY)
    grid = jnp.zeros((9, NZE + 1, NXE + 1, EY + 1), jnp.float32)
    for node in range(8):
        node_z, node_x, node_y = node // 4, (node // 2) % 2, node % 2
        grid = grid.at[:, node_z:node_z + NZE, node_x:node_x + NXE, node_y:node_y + EY].add(terms[:, node])
    nodes = grid[:, :NZE, :NXE, :EY]
    return nodes, gram.reshape(N_GZ, N_XY, EZ, EX, EY, 576)
```

```python
import functools

import jax
import jax.numpy as jnp
import ml_dtypes
import numpy as np
from jax import lax
from jax.experimental import pallas as pl
from jax.experimental.pallas import tpu as pltpu
from jax.sharding import PartitionSpec as P

MESH = pl.DeviceIdType.MESH
CAP = 16
BF = jnp.bfloat16
F32 = jnp.float32
NT = (((1,), (1,)), ((), ()))


def bf16_const(values):
    return np.asarray(values, np.float32).astype(ml_dtypes.bfloat16)


def selection_table():
    where = [(j, k) for j in range(8) for k in range(8)]
    where += [(j, 8) for j in range(8)] + [(8, k) for k in range(8)]
    table = np.zeros((4, 320, 112), np.float32)
    for phase in range(4):
        for shift in range(4):
            for row, (j, k) in enumerate(where):
                src = (j + shift // 2) * 10 + k + shift % 2
                table[phase, shift * 80 + row, phase * 4 + src] = 1.0
    return bf16_const(table)


def slope_table():
    def at(i, j, k):
        if i == 8:
            return 640 + j * 8 + k
        if k == 8:
            return 512 + i * 16 + j
        if j == 8:
            return 512 + i * 16 + 8 + k
        return i * 64 + j * 8 + k

    table = np.zeros((768, 1536), np.float32)
    for i in range(8):
        for j in range(8):
            for k in range(8):
                v = at(i, j, k)
                for c, up in enumerate((at(i + 1, j, k), at(i, j + 1, k), at(i, j, k + 1))):
                    table[up, c * 512 + v] = 1.0
                    table[v, c * 512 + v] = -1.0
    return bf16_const(table)


def split_rows(rows):
    high = bf16_const(rows)
    low = bf16_const(rows - high.astype(np.float64))
    return np.concatenate([high, low], axis=0)


def shape_tables():
    t = (np.arange(8, dtype=np.float64) + 0.5) / 8.0
    rows = []
    for n in range(8):
        az = t if n // 4 else 1.0 - t
        ax = t if n // 2 % 2 else 1.0 - t
        ay = t if n % 2 else 1.0 - t
        rows.append((az[:, None, None] * ax[None, :, None] * ay[None, None, :]).reshape(512))
    shape = np.stack(rows)
    full = (shape[:, None, :] * shape[None, :, :]).reshape(64, 512) / 64.0
    square = shape * shape / 64.0
    gram_rows = np.concatenate([split_rows(full), split_rows(square)], axis=0)
    return gram_rows, split_rows(shape / 64.0)


def exchange_kernel(
    own_ref, idx_ref, cls_ref, brick_ref, sel_ref, out_ref,
    t0, t1, merged, t2, tgt, lhs, wide, send, recv, acc,
    s1, r1, s2, r2, ss, rs,
):
    a = lax.axis_index("gz")
    b = lax.axis_index("xy")
    y, z, x = lax.div(b, 16), lax.rem(lax.div(b, 4), 4), lax.rem(b, 4)
    core = [a, 1 - a]
    x_up = [lax.rem(x + d, 4) for d in range(4)]
    y_up = [lax.rem(y + d, 4) for d in range(4)]
    z_up = [lax.rem(z + d, 4) for d in range(4)]
    line = [(core[p // 4], y * 16 + z * 4 + x_up[p % 4]) for p in range(8)]
    plane = [(a, y_up[q // 4] * 16 + z_up[q % 4] * 4 + x) for q in range(16)]

    barrier = pltpu.get_barrier_semaphore()
    for peer in line[1:] + plane[1:]:
        pl.semaphore_signal(barrier, inc=1, device_id=peer, device_id_type=MESH)

    def row_of(ref):
        return jnp.concatenate([ref[i] for i in range(4)], axis=1)

    owner, wanted, classes = row_of(own_ref), row_of(idx_ref), row_of(cls_ref)
    off_core = ((owner >> 6) + a) & 1
    off_y = ((owner >> 4) - y) & 3
    off_z = ((owner >> 2) - z) & 3
    off_x = (owner - x) & 3
    p_of = off_core * 4 + off_x
    q_of = off_y * 4 + off_z
    sub = lax.broadcasted_iota(jnp.int32, (128, 512), 0)
    hit = sub == p_of * 16 + q_of
    onehot = hit.astype(F32).astype(BF)
    before = (
        lax.broadcasted_iota(jnp.int32, (512, 512), 0)
        < lax.broadcasted_iota(jnp.int32, (512, 512), 1)
    ).astype(F32).astype(BF)
    ahead = jnp.dot(onehot, before, preferred_element_type=F32)
    slot = jnp.sum(jnp.where(hit, ahead, 0.0), axis=0, keepdims=True).astype(jnp.int32)
    target = (q_of * 8 + p_of) * CAP + slot
    tgt[...] = jnp.broadcast_to(target, (128, 512)).T
    in_slot = (sub & 15) == slot
    low = jnp.where(in_slot, wanted & 255, 0).astype(F32).astype(BF)
    high = jnp.where(in_slot, (wanted >> 8) + 2 * classes, 0).astype(F32).astype(BF)
    table = lax.dot_general(
        onehot, jnp.concatenate([low, high], axis=0), NT, preferred_element_type=F32
    )
    table = (table[:, :128] + 256.0 * table[:, 128:]).astype(jnp.int32)
    group = lax.broadcasted_iota(jnp.int32, (128, 128), 0) >> 4
    lane = lax.broadcasted_iota(jnp.int32, (128, 128), 1)
    t0[...] = jnp.where((lane >> 4) == group, table, 0).reshape(8, 16, 128)

    pl.semaphore_wait(barrier, 22)
    first = []
    for p in range(1, 8):
        copy = pltpu.make_async_remote_copy(
            t0.at[p], t1.at[p], s1.at[p], r1.at[p], device_id=line[p], device_id_type=MESH
        )
        copy.start()
        first.append(copy)
    t1[0] = t0[0]

    for i in range(10):
        start = 100 * i // 16 * 16
        depth = min(112, 1000 - start)
        window = jnp.concatenate([brick_ref[e, start : start + depth, :] for e in range(4)], axis=1)
        picked = jnp.dot(
            sel_ref[100 * i % 16 // 4, :, :depth], window, preferred_element_type=F32
        ).astype(BF)
        for shift in range(4):
            lhs[i * 80 : i * 80 + 80, shift * 512 : shift * 512 + 512] = picked[
                shift * 80 : shift * 80 + 80
            ]
    wide[704:768, :] = jnp.zeros((64, 128), BF)

    for copy in first:
        copy.wait()
    rows = jnp.sum(t1[...], axis=0)
    for q in range(16):
        merged[q] = rows[q : q + 1]
    t2[0] = rows[0:1]

    def second(q):
        return pltpu.make_async_remote_copy(
            merged.at[q], t2.at[q], s2.at[q], r2.at[q], device_id=plane[q], device_id_type=MESH
        )

    for q in range(1, 16):
        second(q).start()

    element = lax.broadcasted_iota(jnp.int32, (512, 128), 0)
    eye = (
        lax.broadcasted_iota(jnp.int32, (128, 128), 0)
        == lax.broadcasted_iota(jnp.int32, (128, 128), 1)
    ).astype(F32).astype(BF)
    x_down = [lax.rem(x + 4 - d, 4) for d in range(4)]

    def serve(step, carry):
        @pl.when(step == 1)
        def _():
            for q in range(1, 16):
                second(q).wait()

        q = lax.rem(step * 5, 16)
        request = t2[q]
        brick = request & 511
        cls = request >> 9
        fz = ((cls >> 4).astype(F32) + 0.5) * 0.25
        fx = (((cls >> 2) & 3).astype(F32) + 0.5) * 0.25
        fy = ((cls & 3).astype(F32) + 0.5) * 0.25
        match = element == brick
        weights = []
        for shift in range(4):
            wx = fx if shift // 2 else 1.0 - fx
            wy = fy if shift % 2 else 1.0 - fy
            weights.append(jnp.where(match, wx * wy, 0.0).astype(BF))
        layers = jnp.dot(lhs[...], jnp.concatenate(weights, axis=0), preferred_element_type=F32)
        for i in range(9):
            here = layers[i * 80 : i * 80 + 80] * (1.0 - fz)
            here = here + (layers[i * 80 + 80 : i * 80 + 160] * fz)
            here = here.astype(BF)
            if i < 8:
                wide[i * 64 : i * 64 + 64, :] = here[:64]
                wide[512 + i * 16 : 528 + i * 16, :] = here[64:]
            else:
                wide[640:704, :] = here[:64]
        send[q] = lax.dot_general(eye, wide[...], NT, preferred_element_type=F32).astype(BF)
        yy = lax.rem(y + 4 - lax.div(q, 4), 4)
        zz = lax.rem(z + 4 - lax.rem(q, 4), 4)
        for p in range(8):
            def go(p=p):
                pltpu.make_async_remote_copy(
                    send.at[q, pl.ds(p * CAP, CAP)],
                    recv.at[q, pl.ds(p * CAP, CAP)],
                    ss.at[q],
                    rs.at[q],
                    device_id=(core[p // 4], yy * 16 + zz * 4 + x_down[p % 4]),
                    device_id_type=MESH,
                ).start()

            if p == 0:
                pl.when(step > 0)(go)
            else:
                go()
        return carry

    lax.fori_loop(0, 16, serve, 0)
    recv[0, :CAP, :] = send[0, :CAP, :]
    acc[...] = jnp.zeros_like(acc)
    lanes = lax.broadcasted_iota(jnp.int32, (512, 128), 1)

    def whole(q, lo):
        part = pl.ds(lo, 128 - lo)
        return pltpu.make_async_remote_copy(
            send.at[q, part], recv.at[q, part], ss.at[q], rs.at[q],
            device_id=line[1], device_id_type=MESH,
        )

    def place(step, carry):
        q = lax.rem(step * 5, 16)

        @pl.when(step == 0)
        def _():
            whole(0, CAP).wait_recv()

        @pl.when(step > 0)
        def _():
            whole(q, 0).wait_recv()

        pick = jnp.where(tgt[...] == lanes + q * 128, 1.0, 0.0).astype(BF)
        acc[...] += jnp.dot(pick, recv[q], preferred_element_type=F32)
        return carry

    lax.fori_loop(0, 16, place, 0)
    out_ref[...] = acc[...].astype(BF)
    whole(0, CAP).wait_send()
    for q in range(1, 16):
        whole(q, 0).wait_send()


def exchange(owner, wanted, classes, bricks):
    vmem = pl.BlockSpec(memory_space=pltpu.VMEM)
    dma = pltpu.SemaphoreType.DMA
    return pl.pallas_call(
        exchange_kernel,
        out_shape=jax.ShapeDtypeStruct((512, 768), BF),
        in_specs=[vmem] * 5,
        out_specs=vmem,
        scratch_shapes=[
            pltpu.VMEM((8, 16, 128), jnp.int32),
            pltpu.VMEM((8, 16, 128), jnp.int32),
            pltpu.VMEM((16, 1, 128), jnp.int32),
            pltpu.VMEM((16, 1, 128), jnp.int32),
            pltpu.VMEM((512, 128), jnp.int32),
            pltpu.VMEM((800, 2048), BF),
            pltpu.VMEM((768, 128), BF),
            pltpu.VMEM((16, 128, 768), BF),
            pltpu.VMEM((16, 128, 768), BF),
            pltpu.VMEM((512, 768), F32),
            dma((8,)),
            dma((8,)),
            dma((16,)),
            dma((16,)),
            dma((16,)),
            dma((16,)),
        ],
        compiler_params=pltpu.CompilerParams(
            collective_id=0, has_side_effects=True, vmem_limit_bytes=40 << 20
        ),
    )(owner, wanted, classes, bricks, jnp.asarray(selection_table()))


PAIRS = ((0, 0), (0, 1), (0, 2), (1, 1), (1, 2), (2, 2))


def assemble_kernel(w_ref, img_ref, slope_ref, gram_tab, force_tab, gram_ref, own_ref, face_ref):
    lane = lax.broadcasted_iota(jnp.int32, (8, 128), 1)
    own = [None] * 5
    face = [None] * 5

    def add(old, new):
        return new if old is None else [u + v for u, v in zip(old, new)]

    for e in range(4):
        w = w_ref[e * 128 : e * 128 + 128, :]
        g = jnp.dot(w, slope_ref[...], preferred_element_type=F32)
        g = [g[:, c * 512 : c * 512 + 512] for c in range(3)]
        r = w[:, :512].astype(F32) - img_ref[e * 128 : e * 128 + 128, :].astype(F32)
        products = jnp.concatenate([(g[c] * g[d]).astype(BF) for c, d in PAIRS], axis=0)
        forces = jnp.concatenate([(g[c] * r).astype(BF) for c in range(3)], axis=0)
        sums = lax.dot_general(gram_tab[...], products, NT, preferred_element_type=F32)
        full = sums[:64] + sums[64:128]
        square = sums[128:136] + sums[136:144]
        force = lax.dot_general(force_tab[...], forces, NT, preferred_element_type=F32)
        force = force[:8] + force[8:]
        for c in range(3):
            for d in range(3):
                at = PAIRS.index((min(c, d), max(c, d))) * 128
                for n in range(8):
                    row = (c * 8 + n) * 24 + d * 8
                    gram_ref[e, row : row + 8, :] = full[n * 8 : n * 8 + 8, at : at + 128]
        terms = [force[:, c * 128 : c * 128 + 128] for c in range(3)]
        terms += [square[:, c * 128 : c * 128 + 128] for c in range(6)]
        both = []
        for t in terms:
            moved = jnp.where(lane == 0, 0.0, pltpu.roll(t, 1, 1))
            both.append(t + pltpu.roll(moved, 7, 0))
        own[e] = add(own[e], [t[0:1] for t in both])
        face[e] = add(face[e], [t[2:3] for t in both])
        own[e + 1] = [t[4:5] for t in both]
        face[e + 1] = [t[6:7] for t in both]
    for e in range(5):
        for c in range(9):
            own_ref[c, e : e + 1, :] = own[e][c]
            face_ref[c, e : e + 1, :] = face[e][c]


def assemble(samples, image):
    vmem = pl.BlockSpec(memory_space=pltpu.VMEM)
    gram_rows, force_rows = shape_tables()
    return pl.pallas_call(
        assemble_kernel,
        out_shape=(
            jax.ShapeDtypeStruct((4, 576, 128), F32),
            jax.ShapeDtypeStruct((9, 5, 128), F32),
            jax.ShapeDtypeStruct((9, 5, 128), F32),
        ),
        in_specs=[vmem] * 5,
        out_specs=(vmem,) * 3,
        compiler_params=pltpu.CompilerParams(vmem_limit_bytes=40 << 20),
    )(
        samples,
        image,
        jnp.asarray(slope_table()),
        jnp.asarray(gram_rows),
        jnp.asarray(force_rows),
    )


def passed_along(x, axis):
    size = lax.axis_size(axis)
    return lax.ppermute(x, axis, [(i, i + 1) for i in range(size - 1)])


def per_device(image, bricks, owner, brick_index, offset_class):
    bricks = jnp.transpose(bricks.reshape(4, 128, 1000), (0, 2, 1))
    samples = exchange(
        owner.reshape(4, 1, 128),
        brick_index.reshape(4, 1, 128),
        offset_class.reshape(4, 1, 128),
        bricks,
    )
    gram, own, face = assemble(samples, image.reshape(512, 512))
    own = own + passed_along(face, "xy")
    lid = passed_along(own[:, 4, :], "gz")
    nodes = own[:, :4, :].at[:, 0, :].add(lid).reshape(9, 4, 1, 128)
    return (nodes, jnp.transpose(gram, (0, 2, 1)).reshape(1, 1, 4, 1, 128, 576))


def solution(mesh):
    wide = P("gz", "xy", None, None, None, None)
    narrow = P("gz", "xy", None, None, None)
    return jax.shard_map(
        per_device,
        mesh=mesh,
        in_specs=(wide, wide, wide, narrow, narrow),
        out_specs=(P(None, "gz", "xy", None), wide),
        check_vma=False,
    )
```

```python
import jax
import jax.numpy as jnp
import ml_dtypes
import numpy as np
from jax import lax
from jax.experimental import pallas as pl
from jax.experimental.pallas import tpu as pltpu
from jax.sharding import PartitionSpec as P

MESH = pl.DeviceIdType.MESH
CAP = 16
BF = jnp.bfloat16
F32 = jnp.float32
NT = (((1,), (1,)), ((), ()))


def bf16_const(values):
    return np.asarray(values, np.float32).astype(ml_dtypes.bfloat16)


def selection_table():
    where = [(j, k) for j in range(8) for k in range(8)]
    where += [(j, 8) for j in range(8)] + [(8, k) for k in range(8)]
    table = np.zeros((4, 320, 128), np.float32)
    for phase in range(4):
        for shift in range(4):
            for row, (j, k) in enumerate(where):
                src = (j + shift // 2) * 10 + k + shift % 2
                table[phase, shift * 80 + row, phase * 4 + src] = 1.0
    return bf16_const(table)


def slope_table():
    def at(i, j, k):
        if i == 8:
            return 640 + j * 8 + k
        if k == 8:
            return 512 + i * 16 + j
        if j == 8:
            return 512 + i * 16 + 8 + k
        return i * 64 + j * 8 + k

    table = np.zeros((768, 1536), np.float32)
    for i in range(8):
        for j in range(8):
            for k in range(8):
                v = at(i, j, k)
                for c, up in enumerate((at(i + 1, j, k), at(i, j + 1, k), at(i, j, k + 1))):
                    table[up, c * 512 + v] = 1.0
                    table[v, c * 512 + v] = -1.0
    table[704:] = table[640:704]
    return bf16_const(table)


def split_rows(rows):
    high = bf16_const(rows)
    low = bf16_const(rows - high.astype(np.float64))
    return np.concatenate([high, low], axis=0)


def shape_tables():
    t = (np.arange(8, dtype=np.float64) + 0.5) / 8.0
    rows = []
    for n in range(8):
        az = t if n // 4 else 1.0 - t
        ax = t if n // 2 % 2 else 1.0 - t
        ay = t if n % 2 else 1.0 - t
        rows.append((az[:, None, None] * ax[None, :, None] * ay[None, None, :]).reshape(512))
    shape = np.stack(rows)
    full = (shape[:, None, :] * shape[None, :, :]).reshape(64, 512) / 64.0
    square = shape * shape / 64.0
    return np.concatenate([split_rows(full), split_rows(square), split_rows(shape / 64.0)], axis=0)


PAIRS = ((0, 0), (0, 1), (0, 2), (1, 1), (1, 2), (2, 2))
ROWS = 88


def kernel(
    own_hbm, idx_hbm, cls_hbm, brick_hbm, sel_hbm, img_hbm, slope_hbm, shape_hbm, nodes_ref, gram_ref,
    own_ref, idx_ref, cls_ref, brick_ref, sel_ref, img_ref, slope_ref, shape_ref, loaded,
    t0, t1, merged, t2, tgt, lhs, wide, send, recv, acc, full, part, face_in, lid_in, edge_in,
    s1, r1, s2, r2, ss, rs, hs, hr,
):
    a = lax.axis_index("gz")
    b = lax.axis_index("xy")
    y, z, x = lax.div(b, 16), lax.rem(lax.div(b, 4), 4), lax.rem(b, 4)
    core = [a, 1 - a]
    x_up = [lax.rem(x + d, 4) for d in range(4)]
    y_up = [lax.rem(y + d, 4) for d in range(4)]
    z_up = [lax.rem(z + d, 4) for d in range(4)]
    line = [(core[p // 4], y * 16 + z * 4 + x_up[p % 4]) for p in range(8)]
    plane = [(a, y_up[q // 4] * 16 + z_up[q % 4] * 4 + x) for q in range(16)]

    loads = []
    for n, (src, dst) in enumerate(
        (
            (own_hbm, own_ref),
            (idx_hbm, idx_ref),
            (cls_hbm, cls_ref),
            (brick_hbm, brick_ref),
            (sel_hbm, sel_ref),
            (img_hbm, img_ref),
            (slope_hbm, slope_ref),
            (shape_hbm, shape_ref),
        )
    ):
        loads.append(pltpu.make_async_copy(src, dst, loaded.at[n]))
        loads[-1].start()
    barrier = pltpu.get_barrier_semaphore()
    for peer in line[1:] + plane[1:]:
        pl.semaphore_signal(barrier, inc=1, device_id=peer, device_id_type=MESH)
    for n in range(3):
        loads[n].wait()

    def row_of(ref):
        return jnp.concatenate([ref[i] for i in range(4)], axis=1)

    owner, wanted, classes = row_of(own_ref), row_of(idx_ref), row_of(cls_ref)
    off_core = ((owner >> 6) + a) & 1
    off_y = ((owner >> 4) - y) & 3
    off_z = ((owner >> 2) - z) & 3
    off_x = (owner - x) & 3
    p_of = off_core * 4 + off_x
    q_of = off_y * 4 + off_z
    sub = lax.broadcasted_iota(jnp.int32, (128, 512), 0)
    hit = sub == p_of * 16 + q_of
    onehot = hit.astype(F32).astype(BF)
    before = (
        lax.broadcasted_iota(jnp.int32, (512, 512), 0)
        < lax.broadcasted_iota(jnp.int32, (512, 512), 1)
    ).astype(F32).astype(BF)
    ahead = jnp.dot(onehot, before, preferred_element_type=F32)
    slot = jnp.sum(jnp.where(hit, ahead, 0.0), axis=0, keepdims=True).astype(jnp.int32)
    target = (q_of * 8 + p_of) * CAP + slot
    tgt[...] = jnp.broadcast_to(target, (128, 512)).T
    in_slot = (sub & 15) == slot
    low = jnp.where(in_slot, wanted & 255, 0).astype(F32).astype(BF)
    high = jnp.where(in_slot, (wanted >> 8) + 2 * classes, 0).astype(F32).astype(BF)
    table = lax.dot_general(
        onehot, jnp.concatenate([low, high], axis=0), NT, preferred_element_type=F32
    )
    table = (table[:, :128] + 256.0 * table[:, 128:]).astype(jnp.int32)
    group = lax.broadcasted_iota(jnp.int32, (128, 128), 0) >> 4
    lane = lax.broadcasted_iota(jnp.int32, (128, 128), 1)
    t0[...] = jnp.where((lane >> 4) == group, table, 0).reshape(8, 16, 128)

    pl.semaphore_wait(barrier, 22)
    first = []
    for p in range(1, 8):
        copy = pltpu.make_async_remote_copy(
            t0.at[p], t1.at[p], s1.at[p], r1.at[p], device_id=line[p], device_id_type=MESH
        )
        copy.start()
        first.append(copy)
    t1[0] = t0[0]

    loads[3].wait()
    loads[4].wait()
    for i in range(10):
        start = 100 * i // 16 * 16
        depth = min(112, 1000 - start)
        window = jnp.concatenate([brick_ref[e, start : start + depth, :] for e in range(4)], axis=1)
        picked = jnp.dot(
            sel_ref[100 * i % 16 // 4, :, :depth], window, preferred_element_type=F32
        ).astype(BF)
        for shift in range(4):
            lhs[i * 80 : i * 80 + 80, shift * 512 : shift * 512 + 512] = picked[
                shift * 80 : shift * 80 + 80
            ]

    for copy in first:
        copy.wait()
    rows = jnp.sum(t1[...], axis=0)
    for q in range(16):
        merged[q] = rows[q : q + 1]
    t2[0] = rows[0:1]

    def second(q, to=line[1]):
        return pltpu.make_async_remote_copy(
            merged.at[q], t2.at[q], s2.at[q], r2.at[q], device_id=to, device_id_type=MESH
        )

    for q in range(1, 16):
        second(q, plane[q]).start()

    element = lax.broadcasted_iota(jnp.int32, (512, 128), 0)
    eye = (
        lax.broadcasted_iota(jnp.int32, (128, 128), 0)
        == lax.broadcasted_iota(jnp.int32, (128, 128), 1)
    ).astype(F32).astype(BF)
    x_down = [lax.rem(x + 4 - d, 4) for d in range(4)]

    def serve(step, carry):
        q = lax.rem(step * 5, 16)

        @pl.when(step > 0)
        def _():
            second(q).wait_recv()

        request = t2[q]
        brick = request & 511
        cls = request >> 9
        fz = ((cls >> 4).astype(F32) + 0.5) * 0.25
        fx = (((cls >> 2) & 3).astype(F32) + 0.5) * 0.25
        fy = ((cls & 3).astype(F32) + 0.5) * 0.25
        match = element == brick
        weights = []
        for shift in range(4):
            wx = fx if shift // 2 else 1.0 - fx
            wy = fy if shift % 2 else 1.0 - fy
            weights.append(jnp.where(match, wx * wy, 0.0).astype(BF))
        layers = jnp.dot(lhs[...], jnp.concatenate(weights, axis=0), preferred_element_type=F32)
        for i in range(9):
            here = layers[i * 80 : i * 80 + 80] * (1.0 - fz)
            here = here + (layers[i * 80 + 80 : i * 80 + 160] * fz)
            here = here.astype(BF)
            if i < 8:
                wide[i * 64 : i * 64 + 64, :] = here[:64]
                wide[512 + i * 16 : 528 + i * 16, :] = here[64:]
            else:
                wide[640:704, :] = here[:64]
                wide[704:768, :] = here[:64]
        rows = lax.dot_general(eye, wide[...], NT, preferred_element_type=F32)
        for p in range(8):
            top = p * CAP
            for t in range(5):
                send[q, p, t * CAP : t * CAP + CAP, :] = rows[
                    top : top + CAP, t * 128 : t * 128 + 128
                ].astype(BF)
            send[q, p, 80:ROWS, :] = jnp.where(
                half, rows[top : top + 8, 640:768], rows[top + 8 : top + 16, 640:768]
            ).astype(BF)
        yy = lax.rem(y + 4 - lax.div(q, 4), 4)
        zz = lax.rem(z + 4 - lax.rem(q, 4), 4)
        for p in range(8):

            def go(p=p):
                pltpu.make_async_remote_copy(
                    send.at[q, p],
                    recv.at[q, p],
                    ss.at[q],
                    rs.at[q],
                    device_id=(core[p // 4], yy * 16 + zz * 4 + x_down[p % 4]),
                    device_id_type=MESH,
                ).start()

            if p == 0:
                pl.when(step > 0)(go)
            else:
                go()
        return carry

    half = lax.broadcasted_iota(jnp.int32, (8, 128), 1) < 64
    lax.fori_loop(0, 16, serve, 0)
    recv[0, 0] = send[0, 0]
    acc[...] = jnp.zeros_like(acc)
    lanes = lax.broadcasted_iota(jnp.int32, (512, 128), 1)

    def whole(q, lo):
        group = pl.ds(lo, 8 - lo)
        return pltpu.make_async_remote_copy(
            send.at[q, group], recv.at[q, group], ss.at[q], rs.at[q],
            device_id=line[1], device_id_type=MESH,
        )

    def place(step, carry):
        q = lax.rem(step * 5, 16)

        @pl.when(step == 0)
        def _():
            whole(0, 1).wait_recv()

        @pl.when(step > 0)
        def _():
            whole(q, 0).wait_recv()

        pick = jnp.where(tgt[...] == lanes + q * 128, 1.0, 0.0).astype(BF)
        columns = [
            jnp.concatenate([recv[q, p, t * CAP : t * CAP + CAP, :] for p in range(8)], axis=0)
            for t in range(5)
        ]
        last = []
        for p in range(8):
            rest = recv[q, p, 80:ROWS, :].astype(F32)
            last += [jnp.where(half, rest, 0.0), jnp.where(half, 0.0, rest)]
        columns.append(jnp.concatenate(last, axis=0).astype(BF))
        acc[...] += jnp.dot(pick, jnp.concatenate(columns, axis=1), preferred_element_type=F32)
        return carry

    lax.fori_loop(0, 16, place, 0)

    for n in range(5, 8):
        loads[n].wait()
    lane = lax.broadcasted_iota(jnp.int32, (8, 128), 1)
    sums_of = [[None] * 5, [None] * 5]

    def add(old, new):
        return new if old is None else [u + v for u, v in zip(old, new)]

    for e in range(4):
        w = acc[e * 128 : e * 128 + 128, :].astype(BF)
        g = jnp.dot(w, slope_ref[...], preferred_element_type=F32)
        g = [g[:, c * 512 : c * 512 + 512] for c in range(3)]
        r = acc[e * 128 : e * 128 + 128, :512] - img_ref[e * 128 : e * 128 + 128, :].astype(F32)
        products = jnp.concatenate([(g[c] * g[d]).astype(BF) for c, d in PAIRS], axis=0)
        forces = jnp.concatenate([(g[c] * r).astype(BF) for c in range(3)], axis=0)
        sums = lax.dot_general(shape_ref[:144, :], products, NT, preferred_element_type=F32)
        full[e] = sums[:64] + sums[64:128]
        square = sums[128:136] + sums[136:144]
        force = lax.dot_general(shape_ref[144:160, :], forces, NT, preferred_element_type=F32)
        force = force[:8] + force[8:]
        terms = [force[:, c * 128 : c * 128 + 128] for c in range(3)]
        terms += [square[:, c * 128 : c * 128 + 128] for c in range(6)]
        both = []
        for t in terms:
            moved = jnp.where(lane == 0, 0.0, pltpu.roll(t, 1, 1))
            both.append(t + pltpu.roll(moved, 7, 0))
        for nx in range(2):
            sums_of[nx][e] = add(sums_of[nx][e], [t[2 * nx : 2 * nx + 1] for t in both])
            sums_of[nx][e + 1] = [t[4 + 2 * nx : 5 + 2 * nx] for t in both]
    part[...] = jnp.zeros_like(part)
    for nx in range(2):
        for e in range(5):
            for c in range(9):
                part[nx, e, c : c + 1, :] = sums_of[nx][e][c]

    right = lax.rem(b + 1, 64)
    to_face = pltpu.make_async_remote_copy(
        part.at[1, pl.ds(0, 4)], face_in, hs.at[0], hr.at[0], device_id=(a, right), device_id_type=MESH
    )
    to_lid = pltpu.make_async_remote_copy(
        part.at[0, 4], lid_in, hs.at[1], hr.at[1], device_id=(1 - a, b), device_id_type=MESH
    )
    to_edge = pltpu.make_async_remote_copy(
        part.at[1, 4], edge_in, hs.at[2], hr.at[2], device_id=(1 - a, right), device_id_type=MESH
    )
    pl.when(b < 63)(to_face.start)
    pl.when(a == 0)(to_lid.start)
    pl.when((a == 0) & (b < 63))(to_edge.start)
    for e in range(4):
        for c in range(3):
            for d in range(3):
                at = PAIRS.index((min(c, d), max(c, d))) * 128
                for n in range(8):
                    row = (c * 8 + n) * 24 + d * 8
                    gram_ref[e, row : row + 8, :] = full[e, n * 8 : n * 8 + 8, at : at + 128]

    @pl.when(b > 0)
    def _():
        to_face.wait_recv()
        part[0, :4] += face_in[...]

    @pl.when(a == 1)
    def _():
        to_lid.wait_recv()
        part[0, 0] += lid_in[...]

    @pl.when((a == 1) & (b > 0))
    def _():
        to_edge.wait_recv()
        part[0, 0] += edge_in[...]

    for e in range(4):
        for c in range(9):
            nodes_ref[c, e] = part[0, e, c : c + 1, :]
    pl.when(b < 63)(to_face.wait_send)
    pl.when(a == 0)(to_lid.wait_send)
    pl.when((a == 0) & (b < 63))(to_edge.wait_send)
    whole(0, 1).wait_send()
    for q in range(1, 16):
        second(q).wait_send()
        whole(q, 0).wait_send()


def run(owner, wanted, classes, bricks, image):
    vmem = pl.BlockSpec(memory_space=pltpu.VMEM)
    dma = pltpu.SemaphoreType.DMA
    ints = pltpu.VMEM((4, 1, 128), jnp.int32)
    return pl.pallas_call(
        kernel,
        out_shape=(
            jax.ShapeDtypeStruct((9, 4, 1, 128), F32),
            jax.ShapeDtypeStruct((4, 576, 128), F32),
        ),
        in_specs=[pl.BlockSpec(memory_space=pl.ANY)] * 8,
        out_specs=(vmem, vmem),
        scratch_shapes=[
            ints,
            ints,
            ints,
            pltpu.VMEM((4, 1000, 128), BF),
            pltpu.VMEM((4, 320, 128), BF),
            pltpu.VMEM((512, 512), BF),
            pltpu.VMEM((768, 1536), BF),
            pltpu.VMEM((160, 512), BF),
            dma((8,)),
            pltpu.VMEM((8, 16, 128), jnp.int32),
            pltpu.VMEM((8, 16, 128), jnp.int32),
            pltpu.VMEM((16, 1, 128), jnp.int32),
            pltpu.VMEM((16, 1, 128), jnp.int32),
            pltpu.VMEM((512, 128), jnp.int32),
            pltpu.VMEM((800, 2048), BF),
            pltpu.VMEM((768, 128), BF),
            pltpu.VMEM((16, 8, ROWS, 128), BF),
            pltpu.VMEM((16, 8, ROWS, 128), BF),
            pltpu.VMEM((512, 768), F32),
            pltpu.VMEM((4, 64, 768), F32),
            pltpu.VMEM((2, 5, 16, 128), F32),
            pltpu.VMEM((4, 16, 128), F32),
            pltpu.VMEM((16, 128), F32),
            pltpu.VMEM((16, 128), F32),
            dma((8,)),
            dma((8,)),
            dma((16,)),
            dma((16,)),
            dma((16,)),
            dma((16,)),
            dma((3,)),
            dma((3,)),
        ],
        compiler_params=pltpu.CompilerParams(
            collective_id=0, has_side_effects=True, vmem_limit_bytes=60 << 20
        ),
    )(
        owner,
        wanted,
        classes,
        bricks,
        jnp.asarray(selection_table()),
        image,
        jnp.asarray(slope_table()),
        jnp.asarray(shape_tables()),
    )


def per_device(image, bricks, owner, brick_index, offset_class):
    bricks = jnp.transpose(bricks.reshape(4, 128, 1000), (0, 2, 1))
    nodes, gram = run(
        owner.reshape(4, 1, 128),
        brick_index.reshape(4, 1, 128),
        offset_class.reshape(4, 1, 128),
        bricks,
        image.reshape(512, 512),
    )
    return (nodes, jnp.transpose(gram, (0, 2, 1)).reshape(1, 1, 4, 1, 128, 576))


def solution(mesh):
    wide = P("gz", "xy", None, None, None, None)
    narrow = P("gz", "xy", None, None, None)
    return jax.shard_map(
        per_device,
        mesh=mesh,
        in_specs=(wide, wide, wide, narrow, narrow),
        out_specs=(P(None, "gz", "xy", None), wide),
        check_vma=False,
    )
```

```python
import jax
import jax.numpy as jnp
import ml_dtypes
import numpy as np
from jax import lax
from jax.experimental import pallas as pl
from jax.experimental.pallas import tpu as pltpu
from jax.sharding import PartitionSpec as P

MESH = pl.DeviceIdType.MESH
CAP = 16
BF = jnp.bfloat16
F32 = jnp.float32
NT = (((1,), (1,)), ((), ()))


def bf16_const(values):
    return np.asarray(values, np.float32).astype(ml_dtypes.bfloat16)


def selection_table():
    where = [(j, k) for j in range(8) for k in range(8)]
    where += [(j, 8) for j in range(8)] + [(8, k) for k in range(8)]
    table = np.zeros((4, 320, 128), np.float32)
    for phase in range(4):
        for shift in range(4):
            for row, (j, k) in enumerate(where):
                src = (j + shift // 2) * 10 + k + shift % 2
                table[phase, shift * 80 + row, phase * 4 + src] = 1.0
    return bf16_const(table)


BLOCKS = ((0, 1), (1, 2), (0, 2), (1, 2), (0, 2), (1, 2))


def slope_table():
    def at(i, j, k):
        if i == 8:
            return 640 + j * 8 + k
        if k == 8:
            return 512 + i * 16 + j
        if j == 8:
            return 512 + i * 16 + 8 + k
        return i * 64 + j * 8 + k

    table = np.zeros((768, 1536), np.float32)
    for i in range(8):
        for j in range(8):
            for k in range(8):
                v = at(i, j, k)
                for c, up in enumerate((at(i + 1, j, k), at(i, j + 1, k), at(i, j, k + 1))):
                    table[up, c * 512 + v] = 1.0
                    table[v, c * 512 + v] = -1.0
    table[704:] = table[640:704]
    blocks = []
    for n, (one, two) in enumerate(BLOCKS):
        columns = table[:, n * 256 : n * 256 + 256]
        blocks.append(
            np.concatenate([columns[one * 256 : one * 256 + 256], columns[two * 256 : two * 256 + 256]])
        )
    return bf16_const(np.stack(blocks))


def split_rows(rows):
    high = bf16_const(rows)
    low = bf16_const(rows - high.astype(np.float64))
    return np.concatenate([high, low], axis=0)


def shape_tables():
    t = (np.arange(8, dtype=np.float64) + 0.5) / 8.0
    rows = []
    for n in range(8):
        az = t if n // 4 else 1.0 - t
        ax = t if n // 2 % 2 else 1.0 - t
        ay = t if n % 2 else 1.0 - t
        rows.append((az[:, None, None] * ax[None, :, None] * ay[None, None, :]).reshape(512))
    shape = np.stack(rows)
    full = (shape[:, None, :] * shape[None, :, :]).reshape(64, 512) / 64.0
    square = shape * shape / 64.0
    return np.concatenate([split_rows(full), split_rows(square), split_rows(shape / 64.0)], axis=0)


PAIRS = ((0, 0), (0, 1), (0, 2), (1, 1), (1, 2), (2, 2))
LINE = 128
LAG = 3
ROWS = 88


def kernel(
    own_hbm, idx_hbm, cls_hbm, brick_hbm, sel_hbm, img_hbm, slope_hbm, shape_hbm, nodes_hbm, gram_hbm,
    own_ref, idx_ref, cls_ref, brick_ref, sel_ref, img_ref, slope_ref, shape_ref, loaded,
    t0, t1, merged, t2, tgt, lhs, wide, send_line, recv_line, send, recv, acc,
    gram, nodes, part, face_in, lid_in, edge_in,
    s1, r1, s2, r2, sl, rl, ss, rs, hs, hr, stored,
):
    a = lax.axis_index("gz")
    b = lax.axis_index("xy")
    y, z, x = lax.div(b, 16), lax.rem(lax.div(b, 4), 4), lax.rem(b, 4)
    core = [a, 1 - a]
    x_up = [lax.rem(x + d, 4) for d in range(4)]
    y_up = [lax.rem(y + d, 4) for d in range(4)]
    z_up = [lax.rem(z + d, 4) for d in range(4)]
    line = [(core[p // 4], y * 16 + z * 4 + x_up[p % 4]) for p in range(8)]
    plane = [(a, y_up[q // 4] * 16 + z_up[q % 4] * 4 + x) for q in range(16)]

    loads = []
    for n, (src, dst) in enumerate(
        (
            (own_hbm, own_ref),
            (idx_hbm, idx_ref),
            (cls_hbm, cls_ref),
            (brick_hbm, brick_ref),
            (sel_hbm, sel_ref),
            (img_hbm, img_ref),
            (slope_hbm, slope_ref),
            (shape_hbm, shape_ref),
        )
    ):
        loads.append(pltpu.make_async_copy(src, dst, loaded.at[n]))
    for n in range(5):
        loads[n].start()
    barrier = pltpu.get_barrier_semaphore()
    for peer in line[1:] + plane[1:]:
        pl.semaphore_signal(barrier, inc=1, device_id=peer, device_id_type=MESH)
    for n in range(3):
        loads[n].wait()

    def row_of(ref):
        return jnp.concatenate([ref[i] for i in range(4)], axis=1)

    owner, wanted, classes = row_of(own_ref), row_of(idx_ref), row_of(cls_ref)
    off_core = ((owner >> 6) + a) & 1
    off_y = ((owner >> 4) - y) & 3
    off_z = ((owner >> 2) - z) & 3
    off_x = (owner - x) & 3
    p_of = off_core * 4 + off_x
    q_of = off_y * 4 + off_z
    sub = lax.broadcasted_iota(jnp.int32, (128, 512), 0)
    hit = sub == p_of * 16 + q_of
    onehot = hit.astype(F32).astype(BF)
    before = (
        lax.broadcasted_iota(jnp.int32, (512, 512), 0)
        < lax.broadcasted_iota(jnp.int32, (512, 512), 1)
    ).astype(F32).astype(BF)
    ahead = jnp.dot(onehot, before, preferred_element_type=F32)
    slot = jnp.sum(jnp.where(hit, ahead, 0.0), axis=0, keepdims=True).astype(jnp.int32)
    jy = (off_y - off_x) & 3
    jz = (off_z - 2 * off_core - off_x) & 3
    message = (jy * 2 + (jz >> 1)) * 16 + (jz & 1) * 8 + p_of
    target = jnp.where(q_of == 0, LINE + p_of, message) * CAP + slot
    tgt[...] = jnp.broadcast_to(target, (128, 512)).T
    in_slot = (sub & 15) == slot
    low = jnp.where(in_slot, wanted & 255, 0).astype(F32).astype(BF)
    high = jnp.where(in_slot, (wanted >> 8) + 2 * classes, 0).astype(F32).astype(BF)
    table = lax.dot_general(
        onehot, jnp.concatenate([low, high], axis=0), NT, preferred_element_type=F32
    )
    table = (table[:, :128] + 256.0 * table[:, 128:]).astype(jnp.int32)
    group = lax.broadcasted_iota(jnp.int32, (128, 128), 0) >> 4
    lane = lax.broadcasted_iota(jnp.int32, (128, 128), 1)
    t0[...] = jnp.where((lane >> 4) == group, table, 0).reshape(8, 16, 128)

    pl.semaphore_wait(barrier, 22)
    first = []
    for p in range(1, 8):
        copy = pltpu.make_async_remote_copy(
            t0.at[p], t1.at[p], s1.at[p], r1.at[p], device_id=line[p], device_id_type=MESH
        )
        copy.start()
        first.append(copy)
    t1[0] = t0[0]
    for n in range(5, 8):
        loads[n].start()

    loads[3].wait()
    loads[4].wait()
    for i in range(10):
        start = 100 * i // 16 * 16
        depth = min(112, 1000 - start)
        window = jnp.concatenate([brick_ref[e, start : start + depth, :] for e in range(4)], axis=1)
        picked = jnp.dot(
            sel_ref[100 * i % 16 // 4, :, :depth], window, preferred_element_type=F32
        ).astype(BF)
        for shift in range(4):
            lhs[i * 80 : i * 80 + 80, shift * 512 : shift * 512 + 512] = picked[
                shift * 80 : shift * 80 + 80
            ]

    for p in range(8):
        jy, jz = -(p % 4) % 4, (-2 * (p // 4) - p % 4) % 4
        recv[jy * 2 + jz // 2, jz % 2 * 8 + p] = jnp.zeros((ROWS, 128), BF)
    acc[...] = jnp.zeros_like(acc)
    for copy in first:
        copy.wait_recv()
    rows = jnp.sum(t1[...], axis=0)
    for q in range(16):
        merged[q] = rows[q : q + 1]
    t2[0] = rows[0:1]

    def second(q, to=line[1]):
        return pltpu.make_async_remote_copy(
            merged.at[q], t2.at[q], s2.at[q], r2.at[q], device_id=to, device_id_type=MESH
        )

    for q in range(1, 16):
        second(q, plane[q]).start()

    eye = (
        lax.broadcasted_iota(jnp.int32, (256, 256), 0)
        == lax.broadcasted_iota(jnp.int32, (256, 256), 1)
    ).astype(F32).astype(BF)
    half = lax.broadcasted_iota(jnp.int32, (8, 128), 1) < 64
    slot_group = lax.broadcasted_iota(jnp.int32, (1, 128), 1) >> 4
    x_down = [lax.rem(x + 4 - d, 4) for d in range(4)]

    def serve(request, out, post):
        width = request.shape[1]
        brick = request & 511
        cls = request >> 9
        fz = ((cls >> 4).astype(F32) + 0.5) * 0.25
        fx = (((cls >> 2) & 3).astype(F32) + 0.5) * 0.25
        fy = ((cls & 3).astype(F32) + 0.5) * 0.25
        match = lax.broadcasted_iota(jnp.int32, (512, width), 0) == brick
        weights = []
        for shift in range(4):
            wx = fx if shift // 2 else 1.0 - fx
            wy = fy if shift % 2 else 1.0 - fy
            weights.append(jnp.where(match, wx * wy, 0.0).astype(BF))
        layers = jnp.dot(lhs[...], jnp.concatenate(weights, axis=0), preferred_element_type=F32)
        for i in range(9):
            here = layers[i * 80 : i * 80 + 80] * (1.0 - fz)
            here = here + layers[i * 80 + 80 : i * 80 + 160] * fz
            here = here.astype(BF)
            if i < 8:
                wide[i * 64 : i * 64 + 64, :width] = here[:64]
                wide[512 + i * 16 : 528 + i * 16, :width] = here[64:]
            else:
                wide[640:704, :width] = here[:64]
                wide[704:768, :width] = here[:64]
        rows = lax.dot_general(
            eye[:width, :width], wide[:, :width], NT, preferred_element_type=F32
        )
        for m in range(width // CAP):
            top = m * CAP
            slab = out(m)
            for t in range(5):
                slab[t * CAP : t * CAP + CAP, :] = rows[
                    top : top + CAP, t * 128 : t * 128 + 128
                ].astype(BF)
            slab[80:ROWS, :] = jnp.where(
                half, rows[top : top + 8, 640:768], rows[top + 8 : top + 16, 640:768]
            ).astype(BF)
            post(m)

    def samples_of(slabs):
        columns = [
            jnp.concatenate([slab[t * CAP : t * CAP + CAP, :] for slab in slabs], axis=0)
            for t in range(5)
        ]
        last = []
        for slab in slabs:
            rest = slab[80:ROWS, :].astype(F32)
            last += [jnp.where(half, rest, 0.0), jnp.where(half, 0.0, rest)]
        columns.append(jnp.concatenate(last, axis=0).astype(BF))
        return jnp.concatenate(columns, axis=1)

    def pick_of(first, width):
        lanes = lax.broadcasted_iota(jnp.int32, (512, 128), 1)
        wanted_at = tgt[...]
        return jnp.concatenate(
            [
                jnp.where(wanted_at == lanes + (first + 128 * n), 1.0, 0.0).astype(BF)
                for n in range(width // 128)
            ],
            axis=1,
        )

    on_line = [
        pltpu.make_async_remote_copy(
            send_line.at[p],
            recv_line.at[p],
            sl.at[p],
            rl.at[p],
            device_id=(core[p // 4], y * 16 + z * 4 + x_down[p % 4]),
            device_id_type=MESH,
        )
        for p in range(1, 8)
    ]
    serve(t2[0], lambda m: send_line.at[m], lambda m: on_line[m - 1].start() if m else None)
    recv_line[0] = send_line[0]
    for q in range(1, 16):
        second(q).wait_recv()

    def all_of(n):
        return pltpu.make_async_remote_copy(
            send.at[n, pl.ds(0, 15)], recv.at[n, pl.ds(0, 15)], ss.at[n], rs.at[n],
            device_id=line[1], device_id_type=MESH,
        )

    def place(n):
        all_of(n).wait_recv()
        rows = jnp.concatenate(
            [samples_of([recv.at[n, g * 8 + p] for p in range(8)]) for g in range(2)], axis=0
        )
        acc[...] += jnp.dot(pick_of(n * 256, 256), rows, preferred_element_type=F32)

    def step(n, carry):
        offsets = []
        request = []
        for g in range(2):
            row = jnp.zeros((1, 128), jnp.int32)
            for p in range(8):
                dy = lax.rem(lax.div(n, 2) + p % 4, 4)
                dz = lax.rem(2 * lax.rem(n, 2) + g + 2 * (p // 4) + p % 4, 4)
                offsets.append((dy, dz))
                row = jnp.where(slot_group == p, t2[dy * 4 + dz], row)
            request.append(row)

        def post(m):
            dy, dz = offsets[m]

            @pl.when(dy + dz > 0)
            def _():
                to = lax.rem(y + 4 - dy, 4) * 16 + lax.rem(z + 4 - dz, 4) * 4 + x_down[m % 4]
                pltpu.make_async_remote_copy(
                    send.at[n, m],
                    recv.at[n, m],
                    ss.at[n],
                    rs.at[n],
                    device_id=(core[m // 4 % 2], to),
                    device_id_type=MESH,
                ).start()

        serve(jnp.concatenate(request, axis=1), lambda m: send.at[n, m], post)

        @pl.when(n >= LAG)
        def _():
            place(n - LAG)

        return carry

    lax.fori_loop(0, 8, step, 0)
    for p in range(1, 8):
        on_line[p - 1].wait_recv()
    rows = samples_of([recv_line.at[p] for p in range(8)])
    acc[...] += jnp.dot(pick_of(LINE * CAP, 128), rows, preferred_element_type=F32)

    def rest(n, carry):
        place(n)
        return carry

    lax.fori_loop(8 - LAG, 8, rest, 0)

    for n in range(5, 8):
        loads[n].wait()
    lane = lax.broadcasted_iota(jnp.int32, (8, 128), 1)
    sums_of = [[None] * 5, [None] * 5]
    stores = []

    def add(old, new):
        return new if old is None else [u + v for u, v in zip(old, new)]

    for e in range(4):
        w = acc[e * 128 : e * 128 + 128, :].astype(BF)
        blocks = [w[:, n * 256 : n * 256 + 256] for n in range(3)]
        g = [
            jnp.dot(
                jnp.concatenate([blocks[one], blocks[two]], axis=1),
                slope_ref[n],
                preferred_element_type=F32,
            )
            for n, (one, two) in enumerate(BLOCKS)
        ]
        g = [jnp.concatenate(g[2 * c : 2 * c + 2], axis=1) for c in range(3)]
        r = acc[e * 128 : e * 128 + 128, :512] - img_ref[e * 128 : e * 128 + 128, :].astype(F32)
        products = jnp.concatenate([(g[c] * g[d]).astype(BF) for c, d in PAIRS], axis=0)
        forces = jnp.concatenate([(g[c] * r).astype(BF) for c in range(3)], axis=0)
        sums = lax.dot_general(shape_ref[:144, :], products, NT, preferred_element_type=F32)
        full = sums[:64] + sums[64:128]
        for c in range(3):
            for d in range(3):
                at = PAIRS.index((min(c, d), max(c, d))) * 128
                for n in range(8):
                    row = (c * 8 + n) * 24 + d * 8
                    gram[e, row : row + 8, :] = full[n * 8 : n * 8 + 8, at : at + 128]
        stores.append(pltpu.make_async_copy(gram.at[e], gram_hbm.at[e], stored.at[e]))
        stores[-1].start()
        square = sums[128:136] + sums[136:144]
        force = lax.dot_general(shape_ref[144:160, :], forces, NT, preferred_element_type=F32)
        force = force[:8] + force[8:]
        terms = [force[:, c * 128 : c * 128 + 128] for c in range(3)]
        terms += [square[:, c * 128 : c * 128 + 128] for c in range(6)]
        both = []
        for t in terms:
            moved = jnp.where(lane == 0, 0.0, pltpu.roll(t, 1, 1))
            both.append(t + pltpu.roll(moved, 7, 0))
        for nx in range(2):
            sums_of[nx][e] = add(sums_of[nx][e], [t[2 * nx : 2 * nx + 1] for t in both])
            sums_of[nx][e + 1] = [t[4 + 2 * nx : 5 + 2 * nx] for t in both]
    part[...] = jnp.zeros_like(part)
    for nx in range(2):
        for e in range(5):
            for c in range(9):
                part[nx, e, c : c + 1, :] = sums_of[nx][e][c]

    right = lax.rem(b + 1, 64)
    to_face = pltpu.make_async_remote_copy(
        part.at[1, pl.ds(0, 4)], face_in, hs.at[0], hr.at[0], device_id=(a, right), device_id_type=MESH
    )
    to_lid = pltpu.make_async_remote_copy(
        part.at[0, 4], lid_in, hs.at[1], hr.at[1], device_id=(1 - a, b), device_id_type=MESH
    )
    to_edge = pltpu.make_async_remote_copy(
        part.at[1, 4], edge_in, hs.at[2], hr.at[2], device_id=(1 - a, right), device_id_type=MESH
    )
    pl.when(b < 63)(to_face.start)
    pl.when(a == 0)(to_lid.start)
    pl.when((a == 0) & (b < 63))(to_edge.start)

    @pl.when(b > 0)
    def _():
        to_face.wait_recv()
        part[0, :4] += face_in[...]

    @pl.when(a == 1)
    def _():
        to_lid.wait_recv()
        part[0, 0] += lid_in[...]

    @pl.when((a == 1) & (b > 0))
    def _():
        to_edge.wait_recv()
        part[0, 0] += edge_in[...]

    for e in range(4):
        for c in range(9):
            nodes[c, e] = part[0, e, c : c + 1, :]
    stores.append(pltpu.make_async_copy(nodes, nodes_hbm, stored.at[4]))
    stores[-1].start()
    pl.when(b < 63)(to_face.wait_send)
    pl.when(a == 0)(to_lid.wait_send)
    pl.when((a == 0) & (b < 63))(to_edge.wait_send)
    for p in range(1, 8):
        first[p - 1].wait_send()
        on_line[p - 1].wait_send()
    for q in range(1, 16):
        second(q).wait_send()
    for n in range(8):
        all_of(n).wait_send()
    for store in stores:
        store.wait()


def copy_kernel(nodes_in, gram_in, nodes_out, gram_out, nodes, gram, came, went):
    moves = [(gram_in.at[e], gram.at[e], gram_out.at[e]) for e in range(4)]
    moves.append((nodes_in, nodes, nodes_out))
    inward = [
        pltpu.make_async_copy(src, mid, came.at[n]) for n, (src, mid, _) in enumerate(moves)
    ]
    outward = [
        pltpu.make_async_copy(mid, dst, went.at[n]) for n, (_, mid, dst) in enumerate(moves)
    ]
    for copy in inward:
        copy.start()
    for before, after in zip(inward, outward):
        before.wait()
        after.start()
    for copy in outward:
        copy.wait()


def run(owner, wanted, classes, bricks, image):
    hbm = pl.BlockSpec(memory_space=pl.ANY)
    dma = pltpu.SemaphoreType.DMA
    ints = pltpu.VMEM((4, 1, 128), jnp.int32)
    outs = (
        jax.ShapeDtypeStruct((9, 4, 1, 128), F32),
        jax.ShapeDtypeStruct((4, 576, 128), F32),
    )
    made = pl.pallas_call(
        kernel,
        out_shape=outs,
        in_specs=[hbm] * 8,
        out_specs=(hbm, hbm),
        scratch_shapes=[
            ints,
            ints,
            ints,
            pltpu.VMEM((4, 1000, 128), BF),
            pltpu.VMEM((4, 320, 128), BF),
            pltpu.VMEM((512, 512), BF),
            pltpu.VMEM((6, 512, 256), BF),
            pltpu.VMEM((160, 512), BF),
            dma((8,)),
            pltpu.VMEM((8, 16, 128), jnp.int32),
            pltpu.VMEM((8, 16, 128), jnp.int32),
            pltpu.VMEM((16, 1, 128), jnp.int32),
            pltpu.VMEM((16, 1, 128), jnp.int32),
            pltpu.VMEM((512, 128), jnp.int32),
            pltpu.VMEM((800, 2048), BF),
            pltpu.VMEM((768, 256), BF),
            pltpu.VMEM((8, ROWS, 128), BF),
            pltpu.VMEM((8, ROWS, 128), BF),
            pltpu.VMEM((8, 16, ROWS, 128), BF),
            pltpu.VMEM((8, 16, ROWS, 128), BF),
            pltpu.VMEM((512, 768), F32),
            pltpu.VMEM((4, 576, 128), F32),
            pltpu.VMEM((9, 4, 1, 128), F32),
            pltpu.VMEM((2, 5, 16, 128), F32),
            pltpu.VMEM((4, 16, 128), F32),
            pltpu.VMEM((16, 128), F32),
            pltpu.VMEM((16, 128), F32),
            dma((8,)),
            dma((8,)),
            dma((16,)),
            dma((16,)),
            dma((8,)),
            dma((8,)),
            dma((8,)),
            dma((8,)),
            dma((3,)),
            dma((3,)),
            dma((5,)),
        ],
        compiler_params=pltpu.CompilerParams(
            collective_id=0, has_side_effects=True, vmem_limit_bytes=60 << 20
        ),
    )(
        owner,
        wanted,
        classes,
        bricks,
        jnp.asarray(selection_table()),
        image,
        jnp.asarray(slope_table()),
        jnp.asarray(shape_tables()),
    )
    return pl.pallas_call(
        copy_kernel,
        out_shape=outs,
        in_specs=[hbm] * 2,
        out_specs=(hbm, hbm),
        scratch_shapes=[
            pltpu.VMEM((9, 4, 1, 128), F32),
            pltpu.VMEM((4, 576, 128), F32),
            dma((5,)),
            dma((5,)),
        ],
        compiler_params=pltpu.CompilerParams(vmem_limit_bytes=60 << 20),
    )(*made)


def per_device(image, bricks, owner, brick_index, offset_class):
    bricks = jnp.transpose(bricks.reshape(4, 128, 1000), (0, 2, 1))
    nodes, gram = run(
        owner.reshape(4, 1, 128),
        brick_index.reshape(4, 1, 128),
        offset_class.reshape(4, 1, 128),
        bricks,
        image.reshape(512, 512),
    )
    return (nodes, jnp.transpose(gram, (0, 2, 1)).reshape(1, 1, 4, 1, 128, 576))


def solution(mesh):
    wide = P("gz", "xy", None, None, None, None)
    narrow = P("gz", "xy", None, None, None)
    return jax.shard_map(
        per_device,
        mesh=mesh,
        in_specs=(wide, wide, wide, narrow, narrow),
        out_specs=(P(None, "gz", "xy", None), wide),
        check_vma=False,
    )
```

```python
import jax
import jax.numpy as jnp
import ml_dtypes
import numpy as np
from jax import lax
from jax.experimental import pallas as pl
from jax.experimental.pallas import tpu as pltpu
from jax.sharding import PartitionSpec as P

MESH = pl.DeviceIdType.MESH
CAP = 16
BF = jnp.bfloat16
F32 = jnp.float32
NT = (((1,), (1,)), ((), ()))


def bf16_const(values):
    return np.asarray(values, np.float32).astype(ml_dtypes.bfloat16)


def selection_table():
    where = [(j, k) for j in range(8) for k in range(8)]
    where += [(j, 8) for j in range(8)] + [(8, k) for k in range(8)]
    table = np.zeros((4, 320, 128), np.float32)
    for phase in range(4):
        for shift in range(4):
            for row, (j, k) in enumerate(where):
                src = (j + shift // 2) * 10 + k + shift % 2
                table[phase, shift * 80 + row, phase * 4 + src] = 1.0
    return bf16_const(table)


BLOCKS = ((0, 1), (1, 2), (0, 2), (1, 2), (0, 2), (1, 2))


def slope_table():
    def at(i, j, k):
        if i == 8:
            return 640 + j * 8 + k
        if k == 8:
            return 512 + i * 16 + j
        if j == 8:
            return 512 + i * 16 + 8 + k
        return i * 64 + j * 8 + k

    table = np.zeros((768, 1536), np.float32)
    for i in range(8):
        for j in range(8):
            for k in range(8):
                v = at(i, j, k)
                for c, up in enumerate((at(i + 1, j, k), at(i, j + 1, k), at(i, j, k + 1))):
                    table[up, c * 512 + v] = 1.0
                    table[v, c * 512 + v] = -1.0
    table[704:] = table[640:704]
    blocks = []
    for n, (one, two) in enumerate(BLOCKS):
        columns = table[:, n * 256 : n * 256 + 256]
        blocks.append(
            np.concatenate([columns[one * 256 : one * 256 + 256], columns[two * 256 : two * 256 + 256]])
        )
    return bf16_const(np.stack(blocks))


def split_rows(rows):
    high = bf16_const(rows)
    low = bf16_const(rows - high.astype(np.float64))
    return np.concatenate([high, low], axis=0)


def shape_tables():
    t = (np.arange(8, dtype=np.float64) + 0.5) / 8.0
    rows = []
    for n in range(8):
        az = t if n // 4 else 1.0 - t
        ax = t if n // 2 % 2 else 1.0 - t
        ay = t if n % 2 else 1.0 - t
        rows.append((az[:, None, None] * ax[None, :, None] * ay[None, None, :]).reshape(512))
    shape = np.stack(rows)
    full = (shape[:, None, :] * shape[None, :, :]).reshape(64, 512) / 64.0
    square = shape * shape / 64.0
    return np.concatenate([split_rows(full), split_rows(square), split_rows(shape / 64.0)], axis=0)


PAIRS = ((0, 0), (0, 1), (0, 2), (1, 1), (1, 2), (2, 2))
LAG = 4
FARTHEST_FIRST = sorted(
    (
        (-min(dy, 4 - dy) - min(dz, 4 - dz) - min(dx, 4 - dx), da, dy, dz, dx)
        for da in range(2)
        for dy in range(4)
        for dz in range(4)
        for dx in range(4)
        if da or dy or dz or dx
    )
)
ROWS = 88


def kernel(
    own_hbm, idx_hbm, cls_hbm, brick_hbm, sel_hbm, img_hbm, slope_hbm, shape_hbm, nodes_hbm, gram_hbm,
    own_ref, idx_ref, cls_ref, brick_ref, sel_ref, img_ref, slope_ref, shape_ref, loaded,
    ask_out, ask_in, tgt, lhs, wide, send, recv, acc,
    gram, nodes, part, face_in, lid_in, edge_in,
    asked, asks, ss, rs, hs, hr, stored,
):
    a = lax.axis_index("gz")
    b = lax.axis_index("xy")
    y, z, x = lax.div(b, 16), lax.rem(lax.div(b, 4), 4), lax.rem(b, 4)
    core = [a, 1 - a]
    x_up = [lax.rem(x + d, 4) for d in range(4)]
    y_up = [lax.rem(y + d, 4) for d in range(4)]
    z_up = [lax.rem(z + d, 4) for d in range(4)]
    x_down = [lax.rem(x + 4 - d, 4) for d in range(4)]

    loads = []
    for n, (src, dst) in enumerate(
        (
            (own_hbm, own_ref),
            (idx_hbm, idx_ref),
            (cls_hbm, cls_ref),
            (brick_hbm, brick_ref),
            (sel_hbm, sel_ref),
            (img_hbm, img_ref),
            (slope_hbm, slope_ref),
            (shape_hbm, shape_ref),
        )
    ):
        loads.append(pltpu.make_async_copy(src, dst, loaded.at[n]))
    for n in range(5):
        loads[n].start()
    barrier = pltpu.get_barrier_semaphore()
    for far, da, dy, dz, dx in FARTHEST_FIRST:
        pl.semaphore_signal(
            barrier,
            inc=1,
            device_id=(core[da], y_up[dy] * 16 + z_up[dz] * 4 + x_up[dx]),
            device_id_type=MESH,
        )
    for n in range(3):
        loads[n].wait()

    def row_of(ref):
        return jnp.concatenate([ref[i] for i in range(4)], axis=1)

    owner, wanted, classes = row_of(own_ref), row_of(idx_ref), row_of(cls_ref)
    off_core = ((owner >> 6) + a) & 1
    off_y = ((owner >> 4) - y) & 3
    off_z = ((owner >> 2) - z) & 3
    off_x = (owner - x) & 3
    p_of = off_core * 4 + off_x
    jy = (off_y - off_x) & 3
    jz = (off_z - 2 * off_core - off_x) & 3
    message = (jy * 2 + (jz >> 1)) * 16 + (jz & 1) * 8 + p_of
    sub = lax.broadcasted_iota(jnp.int32, (128, 512), 0)
    hit = sub == message
    onehot = hit.astype(F32).astype(BF)
    before = (
        lax.broadcasted_iota(jnp.int32, (512, 512), 0)
        < lax.broadcasted_iota(jnp.int32, (512, 512), 1)
    ).astype(F32).astype(BF)
    ahead = jnp.dot(onehot, before, preferred_element_type=F32)
    slot = jnp.sum(jnp.where(hit, ahead, 0.0), axis=0, keepdims=True).astype(jnp.int32)
    target = message * CAP + slot
    tgt[...] = jnp.broadcast_to(target, (128, 512)).T
    in_slot = (sub & 15) == slot
    low = jnp.where(in_slot, wanted & 255, 0).astype(F32).astype(BF)
    high = jnp.where(in_slot, (wanted >> 8) + 2 * classes, 0).astype(F32).astype(BF)
    table = lax.dot_general(
        onehot, jnp.concatenate([low, high], axis=0), NT, preferred_element_type=F32
    )
    table = (table[:, :128] + 256.0 * table[:, 128:]).astype(jnp.int32)
    group = lax.broadcasted_iota(jnp.int32, (128, 128), 0) & 7
    lane = lax.broadcasted_iota(jnp.int32, (128, 128), 1)
    ask_out[...] = jnp.where((lane >> 4) == group, table, 0).reshape(16, 8, 128)

    def offset(n, m):
        dy = lax.rem(lax.div(n, 2) + m % 4, 4)
        dz = lax.rem(2 * lax.rem(n, 2) + m // 8 + 2 * (m // 4 % 2) + m % 4, 4)
        return dy, dz

    def ask(n):
        for m in range(16):
            dy, dz = offset(n, m)
            to = lax.rem(y + dy, 4) * 16 + lax.rem(z + dz, 4) * 4 + x_up[m % 4]

            def go(m=m, to=to):
                at = (2 * n + m // 8, pl.ds(m % 8, 1))
                pltpu.make_async_remote_copy(
                    ask_out.at[at],
                    ask_in.at[at],
                    asked.at[n],
                    asks.at[n],
                    device_id=(core[m // 4 % 2], to),
                    device_id_type=MESH,
                ).start()

            if m:
                go()
            elif not isinstance(n, int):
                pl.when(n > 0)(go)
            elif n:
                go()

    def requests(n):
        at = (pl.ds(2 * n, 2),)
        return pltpu.make_async_remote_copy(
            ask_out.at[at], ask_in.at[at], asked.at[n], asks.at[n],
            device_id=(a, b), device_id_type=MESH,
        )

    def own_step():
        at = (pl.ds(0, 15), pl.ds(0, 1))
        return pltpu.make_async_remote_copy(
            ask_out.at[at], ask_in.at[at], asked.at[0], asks.at[0],
            device_id=(a, b), device_id_type=MESH,
        )

    ask_in[0, 0:1] = ask_out[0, 0:1]
    pl.semaphore_wait(barrier, 127)
    for n in range(4, 8):
        ask(n)
    for n in range(5, 8):
        loads[n].start()

    loads[3].wait()
    loads[4].wait()
    for i in range(10):
        start = 100 * i // 16 * 16
        depth = min(112, 1000 - start)
        window = jnp.concatenate([brick_ref[e, start : start + depth, :] for e in range(4)], axis=1)
        picked = jnp.dot(
            sel_ref[100 * i % 16 // 4, :, :depth], window, preferred_element_type=F32
        ).astype(BF)
        for shift in range(4):
            lhs[i * 80 : i * 80 + 80, shift * 512 : shift * 512 + 512] = picked[
                shift * 80 : shift * 80 + 80
            ]

    acc[...] = jnp.zeros_like(acc)

    eye = (
        lax.broadcasted_iota(jnp.int32, (256, 256), 0)
        == lax.broadcasted_iota(jnp.int32, (256, 256), 1)
    ).astype(F32).astype(BF)
    half = lax.broadcasted_iota(jnp.int32, (8, 128), 1) < 64

    def serve(request, out, post):
        width = request.shape[1]
        brick = request & 511
        cls = request >> 9
        fz = ((cls >> 4).astype(F32) + 0.5) * 0.25
        fx = (((cls >> 2) & 3).astype(F32) + 0.5) * 0.25
        fy = ((cls & 3).astype(F32) + 0.5) * 0.25
        match = lax.broadcasted_iota(jnp.int32, (512, width), 0) == brick
        weights = []
        for shift in range(4):
            wx = fx if shift // 2 else 1.0 - fx
            wy = fy if shift % 2 else 1.0 - fy
            weights.append(jnp.where(match, wx * wy, 0.0).astype(BF))
        layers = jnp.dot(lhs[...], jnp.concatenate(weights, axis=0), preferred_element_type=F32)
        for i in range(9):
            here = layers[i * 80 : i * 80 + 80] * (1.0 - fz)
            here = here + layers[i * 80 + 80 : i * 80 + 160] * fz
            here = here.astype(BF)
            if i < 8:
                wide[i * 64 : i * 64 + 64, :width] = here[:64]
                wide[512 + i * 16 : 528 + i * 16, :width] = here[64:]
            else:
                wide[640:704, :width] = here[:64]
                wide[704:768, :width] = here[:64]
        rows = lax.dot_general(
            eye[:width, :width], wide[:, :width], NT, preferred_element_type=F32
        )
        for m in range(width // CAP):
            top = m * CAP
            slab = out(m)
            for t in range(5):
                slab[t * CAP : t * CAP + CAP, :] = rows[
                    top : top + CAP, t * 128 : t * 128 + 128
                ].astype(BF)
            slab[80:ROWS, :] = jnp.where(
                half, rows[top : top + 8, 640:768], rows[top + 8 : top + 16, 640:768]
            ).astype(BF)
            post(m)

    def samples_of(slabs):
        columns = [
            jnp.concatenate([slab[t * CAP : t * CAP + CAP, :] for slab in slabs], axis=0)
            for t in range(5)
        ]
        last = []
        for slab in slabs:
            rest = slab[80:ROWS, :].astype(F32)
            last += [jnp.where(half, rest, 0.0), jnp.where(half, 0.0, rest)]
        columns.append(jnp.concatenate(last, axis=0).astype(BF))
        return jnp.concatenate(columns, axis=1)

    def pick_of(first, width):
        lanes = lax.broadcasted_iota(jnp.int32, (512, 128), 1)
        wanted_at = tgt[...]
        return jnp.concatenate(
            [
                jnp.where(wanted_at == lanes + (first + 128 * n), 1.0, 0.0).astype(BF)
                for n in range(width // 128)
            ],
            axis=1,
        )

    def all_of(n, lo):
        part = pl.ds(lo, 16 - lo)
        return pltpu.make_async_remote_copy(
            send.at[n, part], recv.at[n, part], ss.at[n], rs.at[n],
            device_id=(a, b), device_id_type=MESH,
        )

    def place(n):
        @pl.when(n == 0)
        def _():
            all_of(0, 1).wait_recv()

        @pl.when(n > 0)
        def _():
            all_of(n, 0).wait_recv()

        rows = jnp.concatenate(
            [samples_of([recv.at[n, g * 8 + p] for p in range(8)]) for g in range(2)], axis=0
        )
        acc[...] += jnp.dot(pick_of(n * 256, 256), rows, preferred_element_type=F32)

    def step(t, carry):
        n = lax.rem(t + 4, 8)
        pl.when(t < 4)(lambda: ask(t))

        @pl.when(n == 0)
        def _():
            own_step().wait_recv()

        @pl.when(n > 0)
        def _():
            requests(n).wait_recv()

        request = [jnp.sum(ask_in[2 * n + g], axis=0, keepdims=True) for g in range(2)]

        def post(m):
            dy, dz = offset(n, m)
            to = lax.rem(y + 4 - dy, 4) * 16 + lax.rem(z + 4 - dz, 4) * 4 + x_down[m % 4]

            def go():
                pltpu.make_async_remote_copy(
                    send.at[n, m],
                    recv.at[n, m],
                    ss.at[n],
                    rs.at[n],
                    device_id=(core[m // 4 % 2], to),
                    device_id_type=MESH,
                ).start()

            if m:
                go()
            else:
                pl.when(n > 0)(go)

        serve(jnp.concatenate(request, axis=1), lambda m: send.at[n, m], post)

        @pl.when(n == 0)
        def _():
            recv[0, 0] = send[0, 0]

        @pl.when(t >= LAG)
        def _():
            place(lax.rem(t + 4 - LAG, 8))

        return carry

    lax.fori_loop(0, 8, step, 0)

    def rest(t, carry):
        place(lax.rem(t + 4, 8))
        return carry

    lax.fori_loop(8 - LAG, 8, rest, 0)

    for n in range(5, 8):
        loads[n].wait()
    lane = lax.broadcasted_iota(jnp.int32, (8, 128), 1)
    sums_of = [[None] * 5, [None] * 5]
    stores = []

    def add(old, new):
        return new if old is None else [u + v for u, v in zip(old, new)]

    for e in range(4):
        w = acc[e * 128 : e * 128 + 128, :].astype(BF)
        blocks = [w[:, n * 256 : n * 256 + 256] for n in range(3)]
        g = [
            jnp.dot(
                jnp.concatenate([blocks[one], blocks[two]], axis=1),
                slope_ref[n],
                preferred_element_type=F32,
            )
            for n, (one, two) in enumerate(BLOCKS)
        ]
        g = [jnp.concatenate(g[2 * c : 2 * c + 2], axis=1) for c in range(3)]
        r = acc[e * 128 : e * 128 + 128, :512] - img_ref[e * 128 : e * 128 + 128, :].astype(F32)
        products = jnp.concatenate([(g[c] * g[d]).astype(BF) for c, d in PAIRS], axis=0)
        forces = jnp.concatenate([(g[c] * r).astype(BF) for c in range(3)], axis=0)
        sums = lax.dot_general(shape_ref[:144, :], products, NT, preferred_element_type=F32)
        full = sums[:64] + sums[64:128]
        for c in range(3):
            for d in range(3):
                at = PAIRS.index((min(c, d), max(c, d))) * 128
                for n in range(8):
                    row = (c * 8 + n) * 24 + d * 8
                    gram[e, row : row + 8, :] = full[n * 8 : n * 8 + 8, at : at + 128]
        stores.append(pltpu.make_async_copy(gram.at[e], gram_hbm.at[e], stored.at[e]))
        stores[-1].start()
        square = sums[128:136] + sums[136:144]
        force = lax.dot_general(shape_ref[144:160, :], forces, NT, preferred_element_type=F32)
        force = force[:8] + force[8:]
        terms = [force[:, c * 128 : c * 128 + 128] for c in range(3)]
        terms += [square[:, c * 128 : c * 128 + 128] for c in range(6)]
        both = []
        for t in terms:
            moved = jnp.where(lane == 0, 0.0, pltpu.roll(t, 1, 1))
            both.append(t + pltpu.roll(moved, 7, 0))
        for nx in range(2):
            sums_of[nx][e] = add(sums_of[nx][e], [t[2 * nx : 2 * nx + 1] for t in both])
            sums_of[nx][e + 1] = [t[4 + 2 * nx : 5 + 2 * nx] for t in both]
    part[...] = jnp.zeros_like(part)
    for nx in range(2):
        for e in range(5):
            for c in range(9):
                part[nx, e, c : c + 1, :] = sums_of[nx][e][c]

    right = lax.rem(b + 1, 64)
    to_face = pltpu.make_async_remote_copy(
        part.at[1, pl.ds(0, 4)], face_in, hs.at[0], hr.at[0], device_id=(a, right), device_id_type=MESH
    )
    to_lid = pltpu.make_async_remote_copy(
        part.at[0, 4], lid_in, hs.at[1], hr.at[1], device_id=(1 - a, b), device_id_type=MESH
    )
    to_edge = pltpu.make_async_remote_copy(
        part.at[1, 4], edge_in, hs.at[2], hr.at[2], device_id=(1 - a, right), device_id_type=MESH
    )
    pl.when(b < 63)(to_face.start)
    pl.when(a == 0)(to_lid.start)
    pl.when((a == 0) & (b < 63))(to_edge.start)

    @pl.when(b > 0)
    def _():
        to_face.wait_recv()
        part[0, :4] += face_in[...]

    @pl.when(a == 1)
    def _():
        to_lid.wait_recv()
        part[0, 0] += lid_in[...]

    @pl.when((a == 1) & (b > 0))
    def _():
        to_edge.wait_recv()
        part[0, 0] += edge_in[...]

    for e in range(4):
        for c in range(9):
            nodes[c, e] = part[0, e, c : c + 1, :]
    stores.append(pltpu.make_async_copy(nodes, nodes_hbm, stored.at[4]))
    stores[-1].start()
    pl.when(b < 63)(to_face.wait_send)
    pl.when(a == 0)(to_lid.wait_send)
    pl.when((a == 0) & (b < 63))(to_edge.wait_send)
    own_step().wait_send()
    all_of(0, 1).wait_send()
    for n in range(1, 8):
        requests(n).wait_send()
        all_of(n, 0).wait_send()
    for store in stores:
        store.wait()


def copy_kernel(nodes_in, gram_in, nodes_out, gram_out, nodes, gram, came, went):
    moves = [(gram_in.at[e], gram.at[e], gram_out.at[e]) for e in range(4)]
    moves.append((nodes_in, nodes, nodes_out))
    inward = [
        pltpu.make_async_copy(src, mid, came.at[n]) for n, (src, mid, _) in enumerate(moves)
    ]
    outward = [
        pltpu.make_async_copy(mid, dst, went.at[n]) for n, (_, mid, dst) in enumerate(moves)
    ]
    for copy in inward:
        copy.start()
    for before, after in zip(inward, outward):
        before.wait()
        after.start()
    for copy in outward:
        copy.wait()


def run(owner, wanted, classes, bricks, image):
    hbm = pl.BlockSpec(memory_space=pl.ANY)
    dma = pltpu.SemaphoreType.DMA
    ints = pltpu.VMEM((4, 1, 128), jnp.int32)
    outs = (
        jax.ShapeDtypeStruct((9, 4, 1, 128), F32),
        jax.ShapeDtypeStruct((4, 576, 128), F32),
    )
    made = pl.pallas_call(
        kernel,
        out_shape=outs,
        in_specs=[hbm] * 8,
        out_specs=(hbm, hbm),
        scratch_shapes=[
            ints,
            ints,
            ints,
            pltpu.VMEM((4, 1000, 128), BF),
            pltpu.VMEM((4, 320, 128), BF),
            pltpu.VMEM((512, 512), BF),
            pltpu.VMEM((6, 512, 256), BF),
            pltpu.VMEM((160, 512), BF),
            dma((8,)),
            pltpu.VMEM((16, 8, 128), jnp.int32),
            pltpu.VMEM((16, 8, 128), jnp.int32),
            pltpu.VMEM((512, 128), jnp.int32),
            pltpu.VMEM((800, 2048), BF),
            pltpu.VMEM((768, 256), BF),
            pltpu.VMEM((8, 16, ROWS, 128), BF),
            pltpu.VMEM((8, 16, ROWS, 128), BF),
            pltpu.VMEM((512, 768), F32),
            pltpu.VMEM((4, 576, 128), F32),
            pltpu.VMEM((9, 4, 1, 128), F32),
            pltpu.VMEM((2, 5, 16, 128), F32),
            pltpu.VMEM((4, 16, 128), F32),
            pltpu.VMEM((16, 128), F32),
            pltpu.VMEM((16, 128), F32),
            dma((8,)),
            dma((8,)),
            dma((8,)),
            dma((8,)),
            dma((3,)),
            dma((3,)),
            dma((5,)),
        ],
        compiler_params=pltpu.CompilerParams(
            collective_id=0, has_side_effects=True, vmem_limit_bytes=60 << 20
        ),
    )(
        owner,
        wanted,
        classes,
        bricks,
        jnp.asarray(selection_table()),
        image,
        jnp.asarray(slope_table()),
        jnp.asarray(shape_tables()),
    )
    return pl.pallas_call(
        copy_kernel,
        out_shape=outs,
        in_specs=[hbm] * 2,
        out_specs=(hbm, hbm),
        scratch_shapes=[
            pltpu.VMEM((9, 4, 1, 128), F32),
            pltpu.VMEM((4, 576, 128), F32),
            dma((5,)),
            dma((5,)),
        ],
        compiler_params=pltpu.CompilerParams(vmem_limit_bytes=60 << 20),
    )(*made)


def per_device(image, bricks, owner, brick_index, offset_class):
    bricks = jnp.transpose(bricks.reshape(4, 128, 1000), (0, 2, 1))
    nodes, gram = run(
        owner.reshape(4, 1, 128),
        brick_index.reshape(4, 1, 128),
        offset_class.reshape(4, 1, 128),
        bricks,
        image.reshape(512, 512),
    )
    return (nodes, jnp.transpose(gram, (0, 2, 1)).reshape(1, 1, 4, 1, 128, 576))


def solution(mesh):
    wide = P("gz", "xy", None, None, None, None)
    narrow = P("gz", "xy", None, None, None)
    return jax.shard_map(
        per_device,
        mesh=mesh,
        in_specs=(wide, wide, wide, narrow, narrow),
        out_specs=(P(None, "gz", "xy", None), wide),
        check_vma=False,
    )
```

```python
import jax
import jax.numpy as jnp
import ml_dtypes
import numpy as np
from jax import lax
from jax.experimental import pallas as pl
from jax.experimental.pallas import tpu as pltpu
from jax.sharding import PartitionSpec as P

MESH = pl.DeviceIdType.MESH
CAP = 16
BF = jnp.bfloat16
F32 = jnp.float32
NT = (((1,), (1,)), ((), ()))


def bf16_const(values):
    return np.asarray(values, np.float32).astype(ml_dtypes.bfloat16)


def selection_table():
    where = [(j, k) for j in range(8) for k in range(8)]
    where += [(j, 8) for j in range(8)] + [(8, k) for k in range(8)]
    table = np.zeros((4, 320, 128), np.float32)
    for phase in range(4):
        for shift in range(4):
            for row, (j, k) in enumerate(where):
                src = (j + shift // 2) * 10 + k + shift % 2
                table[phase, shift * 80 + row, phase * 4 + src] = 1.0
    return bf16_const(table)


BLOCKS = ((0, 1), (1, 2), (0, 2), (1, 2), (0, 2), (1, 2))


def slope_table():
    def at(i, j, k):
        if i == 8:
            return 640 + j * 8 + k
        if k == 8:
            return 512 + i * 16 + j
        if j == 8:
            return 512 + i * 16 + 8 + k
        return i * 64 + j * 8 + k

    table = np.zeros((768, 1536), np.float32)
    for i in range(8):
        for j in range(8):
            for k in range(8):
                v = at(i, j, k)
                for c, up in enumerate((at(i + 1, j, k), at(i, j + 1, k), at(i, j, k + 1))):
                    table[up, c * 512 + v] = 1.0
                    table[v, c * 512 + v] = -1.0
    table[704:] = table[640:704]
    blocks = []
    for n, (one, two) in enumerate(BLOCKS):
        columns = table[:, n * 256 : n * 256 + 256]
        blocks.append(
            np.concatenate([columns[one * 256 : one * 256 + 256], columns[two * 256 : two * 256 + 256]])
        )
    return bf16_const(np.stack(blocks))


def split_rows(rows):
    high = bf16_const(rows)
    low = bf16_const(rows - high.astype(np.float64))
    return np.concatenate([high, low], axis=0)


def shape_tables():
    t = (np.arange(8, dtype=np.float64) + 0.5) / 8.0
    rows = []
    for n in range(8):
        az = t if n // 4 else 1.0 - t
        ax = t if n // 2 % 2 else 1.0 - t
        ay = t if n % 2 else 1.0 - t
        rows.append((az[:, None, None] * ax[None, :, None] * ay[None, None, :]).reshape(512))
    shape = np.stack(rows)
    full = (shape[:, None, :] * shape[None, :, :]).reshape(64, 512) / 64.0
    square = shape * shape / 64.0
    return np.concatenate([split_rows(full), split_rows(square), split_rows(shape / 64.0)], axis=0)


PAIRS = ((0, 0), (0, 1), (0, 2), (1, 1), (1, 2), (2, 2))
LAG = 4
FARTHEST_FIRST = sorted(
    (
        (-min(dy, 4 - dy) - min(dz, 4 - dz) - min(dx, 4 - dx), da, dy, dz, dx)
        for da in range(2)
        for dy in range(4)
        for dz in range(4)
        for dx in range(4)
        if da or dy or dz or dx
    )
)
ROWS = 88


def kernel(
    own_hbm, idx_hbm, cls_hbm, brick_hbm, sel_hbm, img_hbm, slope_hbm, shape_hbm, nodes_hbm, gram_hbm,
    own_ref, idx_ref, cls_ref, brick_ref, sel_ref, img_ref, slope_ref, shape_ref, loaded,
    ask_out, ask_in, tgt, lhs, wide, send, recv, acc,
    gram, nodes, part, face_in, lid_in, edge_in,
    asked, asks, ss, rs, hs, hr, stored,
):
    a = lax.axis_index("gz")
    b = lax.axis_index("xy")
    y, z, x = lax.div(b, 16), lax.rem(lax.div(b, 4), 4), lax.rem(b, 4)
    core = [a, 1 - a]
    x_up = [lax.rem(x + d, 4) for d in range(4)]
    y_up = [lax.rem(y + d, 4) for d in range(4)]
    z_up = [lax.rem(z + d, 4) for d in range(4)]
    x_down = [lax.rem(x + 4 - d, 4) for d in range(4)]

    loads = []
    for n, (src, dst) in enumerate(
        (
            (own_hbm, own_ref),
            (idx_hbm, idx_ref),
            (cls_hbm, cls_ref),
            (brick_hbm, brick_ref),
            (sel_hbm, sel_ref),
            (img_hbm, img_ref),
            (slope_hbm, slope_ref),
            (shape_hbm, shape_ref),
        )
    ):
        loads.append(pltpu.make_async_copy(src, dst, loaded.at[n]))
    for n in range(5):
        loads[n].start()
    barrier = pltpu.get_barrier_semaphore()
    for far, da, dy, dz, dx in FARTHEST_FIRST:
        pl.semaphore_signal(
            barrier,
            inc=1,
            device_id=(core[da], y_up[dy] * 16 + z_up[dz] * 4 + x_up[dx]),
            device_id_type=MESH,
        )
    for n in range(3):
        loads[n].wait()

    def row_of(ref):
        return jnp.concatenate([ref[i] for i in range(4)], axis=1)

    owner, wanted, classes = row_of(own_ref), row_of(idx_ref), row_of(cls_ref)
    off_core = ((owner >> 6) + a) & 1
    off_y = ((owner >> 4) - y) & 3
    off_z = ((owner >> 2) - z) & 3
    off_x = (owner - x) & 3
    p_of = off_core * 4 + off_x
    jy = (off_y - off_x) & 3
    jz = (off_z - 2 * off_core - off_x) & 3
    message = (jy * 2 + (jz >> 1)) * 16 + (jz & 1) * 8 + p_of
    sub = lax.broadcasted_iota(jnp.int32, (128, 512), 0)
    hit = sub == message
    onehot = hit.astype(F32).astype(BF)
    before = (
        lax.broadcasted_iota(jnp.int32, (512, 512), 0)
        < lax.broadcasted_iota(jnp.int32, (512, 512), 1)
    ).astype(F32).astype(BF)
    ahead = jnp.dot(onehot, before, preferred_element_type=F32)
    slot = jnp.sum(jnp.where(hit, ahead, 0.0), axis=0, keepdims=True).astype(jnp.int32)
    target = message * CAP + slot
    tgt[...] = jnp.broadcast_to(target, (128, 512)).T
    in_slot = (sub & 15) == slot
    low = jnp.where(in_slot, wanted & 255, 0).astype(F32).astype(BF)
    high = jnp.where(in_slot, (wanted >> 8) + 2 * classes, 0).astype(F32).astype(BF)
    table = lax.dot_general(
        onehot, jnp.concatenate([low, high], axis=0), NT, preferred_element_type=F32
    )
    table = (table[:, :128] + 256.0 * table[:, 128:]).astype(jnp.int32)
    group = lax.broadcasted_iota(jnp.int32, (128, 128), 0) & 7
    lane = lax.broadcasted_iota(jnp.int32, (128, 128), 1)
    ask_out[...] = jnp.where((lane >> 4) == group, table, 0).reshape(16, 8, 128)

    def offset(n, m):
        dy = lax.rem(lax.div(n, 2) + m % 4, 4)
        dz = lax.rem(2 * lax.rem(n, 2) + m // 8 + 2 * (m // 4 % 2) + m % 4, 4)
        return dy, dz

    def ask(n):
        for m in range(16):
            dy, dz = offset(n, m)
            to = lax.rem(y + dy, 4) * 16 + lax.rem(z + dz, 4) * 4 + x_up[m % 4]

            def go(m=m, to=to):
                at = (2 * n + m // 8, pl.ds(m % 8, 1))
                pltpu.make_async_remote_copy(
                    ask_out.at[at],
                    ask_in.at[at],
                    asked.at[n],
                    asks.at[n],
                    device_id=(core[m // 4 % 2], to),
                    device_id_type=MESH,
                ).start()

            if m:
                go()
            elif not isinstance(n, int):
                pl.when(n > 0)(go)
            elif n:
                go()

    def requests(n):
        at = (pl.ds(2 * n, 2),)
        return pltpu.make_async_remote_copy(
            ask_out.at[at], ask_in.at[at], asked.at[n], asks.at[n],
            device_id=(a, b), device_id_type=MESH,
        )

    def own_step():
        at = (pl.ds(0, 15), pl.ds(0, 1))
        return pltpu.make_async_remote_copy(
            ask_out.at[at], ask_in.at[at], asked.at[0], asks.at[0],
            device_id=(a, b), device_id_type=MESH,
        )

    ask_in[0, 0:1] = ask_out[0, 0:1]
    pl.semaphore_wait(barrier, 127)
    for n in (4, 5, 6):
        ask(n)
    loads[3].wait()
    loads[4].wait()
    for i in range(10):
        start = 100 * i // 16 * 16
        depth = min(112, 1000 - start)
        window = jnp.concatenate([brick_ref[e, start : start + depth, :] for e in range(4)], axis=1)
        picked = jnp.dot(
            sel_ref[100 * i % 16 // 4, :, :depth], window, preferred_element_type=F32
        ).astype(BF)
        for shift in range(4):
            lhs[i * 80 : i * 80 + 80, shift * 512 : shift * 512 + 512] = picked[
                shift * 80 : shift * 80 + 80
            ]

    for n in (7, 0, 1, 2, 3):
        ask(n)
    for n in range(5, 8):
        loads[n].start()

    acc[...] = jnp.zeros_like(acc)

    eye = (
        lax.broadcasted_iota(jnp.int32, (256, 256), 0)
        == lax.broadcasted_iota(jnp.int32, (256, 256), 1)
    ).astype(F32).astype(BF)
    half = lax.broadcasted_iota(jnp.int32, (8, 128), 1) < 64

    def serve(request, out, post):
        width = request.shape[1]
        brick = request & 511
        cls = request >> 9
        fz = ((cls >> 4).astype(F32) + 0.5) * 0.25
        fx = (((cls >> 2) & 3).astype(F32) + 0.5) * 0.25
        fy = ((cls & 3).astype(F32) + 0.5) * 0.25
        match = lax.broadcasted_iota(jnp.int32, (512, width), 0) == brick
        weights = []
        for shift in range(4):
            wx = fx if shift // 2 else 1.0 - fx
            wy = fy if shift % 2 else 1.0 - fy
            weights.append(jnp.where(match, wx * wy, 0.0).astype(BF))
        layers = jnp.dot(lhs[...], jnp.concatenate(weights, axis=0), preferred_element_type=F32)
        for i in range(9):
            here = layers[i * 80 : i * 80 + 80] * (1.0 - fz)
            here = here + layers[i * 80 + 80 : i * 80 + 160] * fz
            here = here.astype(BF)
            if i < 8:
                wide[i * 64 : i * 64 + 64, :width] = here[:64]
                wide[512 + i * 16 : 528 + i * 16, :width] = here[64:]
            else:
                wide[640:704, :width] = here[:64]
                wide[704:768, :width] = here[:64]
        rows = lax.dot_general(
            eye[:width, :width], wide[:, :width], NT, preferred_element_type=F32
        )
        for m in range(width // CAP):
            top = m * CAP
            slab = out(m)
            for t in range(5):
                slab[t * CAP : t * CAP + CAP, :] = rows[
                    top : top + CAP, t * 128 : t * 128 + 128
                ].astype(BF)
            slab[80:ROWS, :] = jnp.where(
                half, rows[top : top + 8, 640:768], rows[top + 8 : top + 16, 640:768]
            ).astype(BF)
            post(m)

    def samples_of(slabs):
        columns = [
            jnp.concatenate([slab[t * CAP : t * CAP + CAP, :] for slab in slabs], axis=0)
            for t in range(5)
        ]
        last = []
        for slab in slabs:
            rest = slab[80:ROWS, :].astype(F32)
            last += [jnp.where(half, rest, 0.0), jnp.where(half, 0.0, rest)]
        columns.append(jnp.concatenate(last, axis=0).astype(BF))
        return jnp.concatenate(columns, axis=1)

    def pick_of(first, width):
        lanes = lax.broadcasted_iota(jnp.int32, (512, 128), 1)
        wanted_at = tgt[...]
        return jnp.concatenate(
            [
                jnp.where(wanted_at == lanes + (first + 128 * n), 1.0, 0.0).astype(BF)
                for n in range(width // 128)
            ],
            axis=1,
        )

    def all_of(n, lo):
        part = pl.ds(lo, 16 - lo)
        return pltpu.make_async_remote_copy(
            send.at[n, part], recv.at[n, part], ss.at[n], rs.at[n],
            device_id=(a, b), device_id_type=MESH,
        )

    def place(n):
        @pl.when(n == 0)
        def _():
            all_of(0, 1).wait_recv()

        @pl.when(n > 0)
        def _():
            all_of(n, 0).wait_recv()

        rows = jnp.concatenate(
            [samples_of([recv.at[n, g * 8 + p] for p in range(8)]) for g in range(2)], axis=0
        )
        acc[...] += jnp.dot(pick_of(n * 256, 256), rows, preferred_element_type=F32)

    def step(t, carry):
        n = lax.rem(t + 4, 8)
        @pl.when(n == 0)
        def _():
            own_step().wait_recv()

        @pl.when(n > 0)
        def _():
            requests(n).wait_recv()

        request = [jnp.sum(ask_in[2 * n + g], axis=0, keepdims=True) for g in range(2)]

        def post(m):
            dy, dz = offset(n, m)
            to = lax.rem(y + 4 - dy, 4) * 16 + lax.rem(z + 4 - dz, 4) * 4 + x_down[m % 4]

            def go():
                pltpu.make_async_remote_copy(
                    send.at[n, m],
                    recv.at[n, m],
                    ss.at[n],
                    rs.at[n],
                    device_id=(core[m // 4 % 2], to),
                    device_id_type=MESH,
                ).start()

            if m:
                go()
            else:
                pl.when(n > 0)(go)

        serve(jnp.concatenate(request, axis=1), lambda m: send.at[n, m], post)

        @pl.when(n == 0)
        def _():
            recv[0, 0] = send[0, 0]

        @pl.when(t >= LAG)
        def _():
            place(lax.rem(t + 4 - LAG, 8))

        return carry

    lax.fori_loop(0, 8, step, 0)

    def rest(t, carry):
        place(lax.rem(t + 4, 8))
        return carry

    lax.fori_loop(8 - LAG, 8, rest, 0)

    for n in range(5, 8):
        loads[n].wait()
    lane = lax.broadcasted_iota(jnp.int32, (8, 128), 1)
    sums_of = [[None] * 5, [None] * 5]
    stores = []

    def add(old, new):
        return new if old is None else [u + v for u, v in zip(old, new)]

    for e in range(4):
        w = acc[e * 128 : e * 128 + 128, :].astype(BF)
        blocks = [w[:, n * 256 : n * 256 + 256] for n in range(3)]
        g = [
            jnp.dot(
                jnp.concatenate([blocks[one], blocks[two]], axis=1),
                slope_ref[n],
                preferred_element_type=F32,
            )
            for n, (one, two) in enumerate(BLOCKS)
        ]
        g = [jnp.concatenate(g[2 * c : 2 * c + 2], axis=1) for c in range(3)]
        r = acc[e * 128 : e * 128 + 128, :512] - img_ref[e * 128 : e * 128 + 128, :].astype(F32)
        products = jnp.concatenate([(g[c] * g[d]).astype(BF) for c, d in PAIRS], axis=0)
        forces = jnp.concatenate([(g[c] * r).astype(BF) for c in range(3)], axis=0)
        sums = lax.dot_general(shape_ref[:144, :], products, NT, preferred_element_type=F32)
        full = sums[:64] + sums[64:128]
        for c in range(3):
            for d in range(3):
                at = PAIRS.index((min(c, d), max(c, d))) * 128
                for n in range(8):
                    row = (c * 8 + n) * 24 + d * 8
                    gram[e, row : row + 8, :] = full[n * 8 : n * 8 + 8, at : at + 128]
        stores.append(pltpu.make_async_copy(gram.at[e], gram_hbm.at[e], stored.at[e]))
        stores[-1].start()
        square = sums[128:136] + sums[136:144]
        force = lax.dot_general(shape_ref[144:160, :], forces, NT, preferred_element_type=F32)
        force = force[:8] + force[8:]
        terms = [force[:, c * 128 : c * 128 + 128] for c in range(3)]
        terms += [square[:, c * 128 : c * 128 + 128] for c in range(6)]
        both = []
        for t in terms:
            moved = jnp.where(lane == 0, 0.0, pltpu.roll(t, 1, 1))
            both.append(t + pltpu.roll(moved, 7, 0))
        for nx in range(2):
            sums_of[nx][e] = add(sums_of[nx][e], [t[2 * nx : 2 * nx + 1] for t in both])
            sums_of[nx][e + 1] = [t[4 + 2 * nx : 5 + 2 * nx] for t in both]
    part[...] = jnp.zeros_like(part)
    for nx in range(2):
        for e in range(5):
            for c in range(9):
                part[nx, e, c : c + 1, :] = sums_of[nx][e][c]

    right = lax.rem(b + 1, 64)
    to_face = pltpu.make_async_remote_copy(
        part.at[1, pl.ds(0, 4)], face_in, hs.at[0], hr.at[0], device_id=(a, right), device_id_type=MESH
    )
    to_lid = pltpu.make_async_remote_copy(
        part.at[0, 4], lid_in, hs.at[1], hr.at[1], device_id=(1 - a, b), device_id_type=MESH
    )
    to_edge = pltpu.make_async_remote_copy(
        part.at[1, 4], edge_in, hs.at[2], hr.at[2], device_id=(1 - a, right), device_id_type=MESH
    )
    pl.when(b < 63)(to_face.start)
    pl.when(a == 0)(to_lid.start)
    pl.when((a == 0) & (b < 63))(to_edge.start)

    @pl.when(b > 0)
    def _():
        to_face.wait_recv()
        part[0, :4] += face_in[...]

    @pl.when(a == 1)
    def _():
        to_lid.wait_recv()
        part[0, 0] += lid_in[...]

    @pl.when((a == 1) & (b > 0))
    def _():
        to_edge.wait_recv()
        part[0, 0] += edge_in[...]

    for e in range(4):
        for c in range(9):
            nodes[c, e] = part[0, e, c : c + 1, :]
    stores.append(pltpu.make_async_copy(nodes, nodes_hbm, stored.at[4]))
    stores[-1].start()
    pl.when(b < 63)(to_face.wait_send)
    pl.when(a == 0)(to_lid.wait_send)
    pl.when((a == 0) & (b < 63))(to_edge.wait_send)
    own_step().wait_send()
    all_of(0, 1).wait_send()
    for n in range(1, 8):
        requests(n).wait_send()
        all_of(n, 0).wait_send()
    for store in stores:
        store.wait()


def copy_kernel(nodes_in, gram_in, nodes_out, gram_out, nodes, gram, came, went):
    moves = [(gram_in.at[e], gram.at[e], gram_out.at[e]) for e in range(4)]
    moves.append((nodes_in, nodes, nodes_out))
    inward = [
        pltpu.make_async_copy(src, mid, came.at[n]) for n, (src, mid, _) in enumerate(moves)
    ]
    outward = [
        pltpu.make_async_copy(mid, dst, went.at[n]) for n, (_, mid, dst) in enumerate(moves)
    ]
    for copy in inward:
        copy.start()
    for before, after in zip(inward, outward):
        before.wait()
        after.start()
    for copy in outward:
        copy.wait()


def run(owner, wanted, classes, bricks, image):
    hbm = pl.BlockSpec(memory_space=pl.ANY)
    dma = pltpu.SemaphoreType.DMA
    ints = pltpu.VMEM((4, 1, 128), jnp.int32)
    outs = (
        jax.ShapeDtypeStruct((9, 4, 1, 128), F32),
        jax.ShapeDtypeStruct((4, 576, 128), F32),
    )
    made = pl.pallas_call(
        kernel,
        out_shape=outs,
        in_specs=[hbm] * 8,
        out_specs=(hbm, hbm),
        scratch_shapes=[
            ints,
            ints,
            ints,
            pltpu.VMEM((4, 1000, 128), BF),
            pltpu.VMEM((4, 320, 128), BF),
            pltpu.VMEM((512, 512), BF),
            pltpu.VMEM((6, 512, 256), BF),
            pltpu.VMEM((160, 512), BF),
            dma((8,)),
            pltpu.VMEM((16, 8, 128), jnp.int32),
            pltpu.VMEM((16, 8, 128), jnp.int32),
            pltpu.VMEM((512, 128), jnp.int32),
            pltpu.VMEM((800, 2048), BF),
            pltpu.VMEM((768, 256), BF),
            pltpu.VMEM((8, 16, ROWS, 128), BF),
            pltpu.VMEM((8, 16, ROWS, 128), BF),
            pltpu.VMEM((512, 768), F32),
            pltpu.VMEM((4, 576, 128), F32),
            pltpu.VMEM((9, 4, 1, 128), F32),
            pltpu.VMEM((2, 5, 16, 128), F32),
            pltpu.VMEM((4, 16, 128), F32),
            pltpu.VMEM((16, 128), F32),
            pltpu.VMEM((16, 128), F32),
            dma((8,)),
            dma((8,)),
            dma((8,)),
            dma((8,)),
            dma((3,)),
            dma((3,)),
            dma((5,)),
        ],
        compiler_params=pltpu.CompilerParams(
            collective_id=0, has_side_effects=True, vmem_limit_bytes=60 << 20
        ),
    )(
        owner,
        wanted,
        classes,
        bricks,
        jnp.asarray(selection_table()),
        image,
        jnp.asarray(slope_table()),
        jnp.asarray(shape_tables()),
    )
    return pl.pallas_call(
        copy_kernel,
        out_shape=outs,
        in_specs=[hbm] * 2,
        out_specs=(hbm, hbm),
        scratch_shapes=[
            pltpu.VMEM((9, 4, 1, 128), F32),
            pltpu.VMEM((4, 576, 128), F32),
            dma((5,)),
            dma((5,)),
        ],
        compiler_params=pltpu.CompilerParams(vmem_limit_bytes=60 << 20),
    )(*made)


def per_device(image, bricks, owner, brick_index, offset_class):
    bricks = jnp.transpose(bricks.reshape(4, 128, 1000), (0, 2, 1))
    nodes, gram = run(
        owner.reshape(4, 1, 128),
        brick_index.reshape(4, 1, 128),
        offset_class.reshape(4, 1, 128),
        bricks,
        image.reshape(512, 512),
    )
    return (nodes, jnp.transpose(gram, (0, 2, 1)).reshape(1, 1, 4, 1, 128, 576))


def solution(mesh):
    wide = P("gz", "xy", None, None, None, None)
    narrow = P("gz", "xy", None, None, None)
    return jax.shard_map(
        per_device,
        mesh=mesh,
        in_specs=(wide, wide, wide, narrow, narrow),
        out_specs=(P(None, "gz", "xy", None), wide),
        check_vma=False,
    )
```

```python
import jax
import jax.numpy as jnp
import ml_dtypes
import numpy as np
from jax import lax
from jax.experimental import pallas as pl
from jax.experimental.pallas import tpu as pltpu
from jax.sharding import PartitionSpec as P

MESH = pl.DeviceIdType.MESH
CAP = 16
BF = jnp.bfloat16
F32 = jnp.float32
NT = (((1,), (1,)), ((), ()))


def bf16_const(values):
    return np.asarray(values, np.float32).astype(ml_dtypes.bfloat16)


def selection_table():
    where = [(j, k) for j in range(8) for k in range(8)]
    where += [(j, 8) for j in range(8)] + [(8, k) for k in range(8)]
    table = np.zeros((4, 320, 128), np.float32)
    for phase in range(4):
        for shift in range(4):
            for row, (j, k) in enumerate(where):
                src = (j + shift // 2) * 10 + k + shift % 2
                table[phase, shift * 80 + row, phase * 4 + src] = 1.0
    return bf16_const(table)


BLOCKS = ((0, 2), (1, 2), (0, 2), (1, 2))


def slope_table():
    def at(i, j, k):
        if k == 8:
            return 512 + i * 16 + j
        if j == 8:
            return 512 + i * 16 + 8 + k
        return i * 64 + j * 8 + k

    table = np.zeros((768, 1024), np.float32)
    for i in range(8):
        for j in range(8):
            for k in range(8):
                v = at(i, j, k)
                for c, up in enumerate((at(i, j + 1, k), at(i, j, k + 1))):
                    table[up, c * 512 + v] = 1.0
                    table[v, c * 512 + v] = -1.0
    blocks = []
    for n, (one, two) in enumerate(BLOCKS):
        columns = table[:, n * 256 : n * 256 + 256]
        blocks.append(
            np.concatenate([columns[one * 256 : one * 256 + 256], columns[two * 256 : two * 256 + 256]])
        )
    return bf16_const(np.stack(blocks))


def split_rows(rows):
    high = bf16_const(rows)
    low = bf16_const(rows - high.astype(np.float64))
    return np.concatenate([high, low], axis=0)


def shape_tables():
    t = (np.arange(8, dtype=np.float64) + 0.5) / 8.0
    rows = []
    for n in range(8):
        az = t if n // 4 else 1.0 - t
        ax = t if n // 2 % 2 else 1.0 - t
        ay = t if n % 2 else 1.0 - t
        rows.append((az[:, None, None] * ax[None, :, None] * ay[None, None, :]).reshape(512))
    shape = np.stack(rows)
    full = (shape[:, None, :] * shape[None, :, :]).reshape(64, 512) / 64.0
    table = np.zeros((2048, 128), ml_dtypes.bfloat16)
    table[:512] = split_rows(full).T
    for c in range(3):
        table[512 + c * 512 : 1024 + c * 512, c * 16 : c * 16 + 16] = split_rows(shape / 64.0).T
    return table


PAIRS = ((0, 0), (0, 1), (0, 2), (1, 1), (1, 2), (2, 2))
LAG = 4
FARTHEST_FIRST = sorted(
    (
        (-min(dy, 4 - dy) - min(dz, 4 - dz) - min(dx, 4 - dx), da, dy, dz, dx)
        for da in range(2)
        for dy in range(4)
        for dz in range(4)
        for dx in range(4)
        if da or dy or dz or dx
    )
)
ROWS = 88


def kernel(
    own_hbm, idx_hbm, cls_hbm, brick_hbm, sel_hbm, img_hbm, slope_hbm, shape_hbm, nodes_hbm, gram_hbm,
    own_ref, idx_ref, cls_ref, brick_ref, sel_ref, img_ref, slope_ref, shape_ref, loaded,
    ask_out, ask_in, tgt, lhs, wide, send, recv, acc,
    gram, nodes, part, face_in, lid_in, edge_in,
    asked, asks, ss, rs, hs, hr, stored,
):
    a = lax.axis_index("gz")
    b = lax.axis_index("xy")
    y, z, x = lax.div(b, 16), lax.rem(lax.div(b, 4), 4), lax.rem(b, 4)
    core = [a, 1 - a]
    x_up = [lax.rem(x + d, 4) for d in range(4)]
    y_up = [lax.rem(y + d, 4) for d in range(4)]
    z_up = [lax.rem(z + d, 4) for d in range(4)]
    x_down = [lax.rem(x + 4 - d, 4) for d in range(4)]

    loads = []
    for n, (src, dst) in enumerate(
        (
            (own_hbm, own_ref),
            (idx_hbm, idx_ref),
            (cls_hbm, cls_ref),
            (brick_hbm, brick_ref),
            (sel_hbm, sel_ref),
            (img_hbm, img_ref),
            (slope_hbm, slope_ref),
            (shape_hbm, shape_ref),
        )
    ):
        loads.append(pltpu.make_async_copy(src, dst, loaded.at[n]))
    for n in range(5):
        loads[n].start()
    barrier = pltpu.get_barrier_semaphore()
    for far, da, dy, dz, dx in FARTHEST_FIRST:
        pl.semaphore_signal(
            barrier,
            inc=1,
            device_id=(core[da], y_up[dy] * 16 + z_up[dz] * 4 + x_up[dx]),
            device_id_type=MESH,
        )
    for n in range(3):
        loads[n].wait()

    def row_of(ref):
        return jnp.concatenate([ref[i] for i in range(4)], axis=1)

    owner, wanted, classes = row_of(own_ref), row_of(idx_ref), row_of(cls_ref)
    off_core = ((owner >> 6) + a) & 1
    off_y = ((owner >> 4) - y) & 3
    off_z = ((owner >> 2) - z) & 3
    off_x = (owner - x) & 3
    p_of = off_core * 4 + off_x
    jy = (off_y - off_x) & 3
    jz = (off_z - 2 * off_core - off_x) & 3
    message = (jy * 2 + (jz >> 1)) * 16 + (jz & 1) * 8 + p_of
    sub = lax.broadcasted_iota(jnp.int32, (128, 512), 0)
    hit = sub == message
    onehot = hit.astype(F32).astype(BF)
    before = (
        lax.broadcasted_iota(jnp.int32, (512, 512), 0)
        < lax.broadcasted_iota(jnp.int32, (512, 512), 1)
    ).astype(F32).astype(BF)
    ahead = jnp.dot(onehot, before, preferred_element_type=F32)
    slot = jnp.sum(jnp.where(hit, ahead, 0.0), axis=0, keepdims=True).astype(jnp.int32)
    target = message * CAP + slot
    tgt[...] = jnp.broadcast_to(target, (128, 512)).T
    in_slot = (sub & 15) == slot
    low = jnp.where(in_slot, wanted & 255, 0).astype(F32).astype(BF)
    high = jnp.where(in_slot, (wanted >> 8) + 2 * classes, 0).astype(F32).astype(BF)
    table = lax.dot_general(
        onehot, jnp.concatenate([low, high], axis=0), NT, preferred_element_type=F32
    )
    table = (table[:, :128] + 256.0 * table[:, 128:]).astype(jnp.int32)
    group = lax.broadcasted_iota(jnp.int32, (128, 128), 0) & 7
    lane = lax.broadcasted_iota(jnp.int32, (128, 128), 1)
    ask_out[...] = jnp.where((lane >> 4) == group, table, 0).reshape(16, 8, 128)

    def offset(n, m):
        dy = lax.rem(lax.div(n, 2) + m % 4, 4)
        dz = lax.rem(2 * lax.rem(n, 2) + m // 8 + 2 * (m // 4 % 2) + m % 4, 4)
        return dy, dz

    def ask(n):
        for m in range(16):
            dy, dz = offset(n, m)
            to = lax.rem(y + dy, 4) * 16 + lax.rem(z + dz, 4) * 4 + x_up[m % 4]

            def go(m=m, to=to):
                at = (2 * n + m // 8, pl.ds(m % 8, 1))
                pltpu.make_async_remote_copy(
                    ask_out.at[at],
                    ask_in.at[at],
                    asked.at[n],
                    asks.at[n],
                    device_id=(core[m // 4 % 2], to),
                    device_id_type=MESH,
                ).start()

            if m:
                go()
            elif not isinstance(n, int):
                pl.when(n > 0)(go)
            elif n:
                go()

    def ask_step(t, carry):
        ask(lax.rem(t, 8))
        return carry

    def requests(n):
        at = (pl.ds(2 * n, 2),)
        return pltpu.make_async_remote_copy(
            ask_out.at[at], ask_in.at[at], asked.at[n], asks.at[n],
            device_id=(a, b), device_id_type=MESH,
        )

    def own_step():
        at = (pl.ds(0, 15), pl.ds(0, 1))
        return pltpu.make_async_remote_copy(
            ask_out.at[at], ask_in.at[at], asked.at[0], asks.at[0],
            device_id=(a, b), device_id_type=MESH,
        )

    ask_in[0, 0:1] = ask_out[0, 0:1]
    pl.semaphore_wait(barrier, 127)
    lax.fori_loop(4, 7, ask_step, 0)
    loads[3].wait()
    loads[4].wait()
    for i in range(10):
        start = 100 * i // 16 * 16
        depth = min(112, 1000 - start)
        window = jnp.concatenate([brick_ref[e, start : start + depth, :] for e in range(4)], axis=1)
        picked = jnp.dot(
            sel_ref[100 * i % 16 // 4, :, :depth], window, preferred_element_type=F32
        ).astype(BF)
        for shift in range(4):
            lhs[i * 80 : i * 80 + 80, shift * 512 : shift * 512 + 512] = picked[
                shift * 80 : shift * 80 + 80
            ]

    lax.fori_loop(7, 12, ask_step, 0)
    for n in range(5, 8):
        loads[n].start()

    acc[...] = jnp.zeros_like(acc)

    eye = (
        lax.broadcasted_iota(jnp.int32, (256, 256), 0)
        == lax.broadcasted_iota(jnp.int32, (256, 256), 1)
    ).astype(F32).astype(BF)
    half = lax.broadcasted_iota(jnp.int32, (8, 128), 1) < 64

    def serve(request, out, post):
        width = request.shape[1]
        brick = request & 511
        cls = request >> 9
        fz = ((cls >> 4).astype(F32) + 0.5) * 0.25
        fx = (((cls >> 2) & 3).astype(F32) + 0.5) * 0.25
        fy = ((cls & 3).astype(F32) + 0.5) * 0.25
        match = lax.broadcasted_iota(jnp.int32, (512, width), 0) == brick
        weights = []
        for shift in range(4):
            wx = fx if shift // 2 else 1.0 - fx
            wy = fy if shift % 2 else 1.0 - fy
            weights.append(jnp.where(match, wx * wy, 0.0).astype(BF))
        layers = jnp.dot(lhs[...], jnp.concatenate(weights, axis=0), preferred_element_type=F32)
        for i in range(9):
            here = layers[i * 80 : i * 80 + 80] * (1.0 - fz)
            here = here + layers[i * 80 + 80 : i * 80 + 160] * fz
            here = here.astype(BF)
            if i < 8:
                wide[i * 64 : i * 64 + 64, :width] = here[:64]
                wide[512 + i * 16 : 528 + i * 16, :width] = here[64:]
            else:
                wide[640:704, :width] = here[:64]
                wide[704:768, :width] = here[:64]
        rows = lax.dot_general(
            eye[:width, :width], wide[:, :width], NT, preferred_element_type=F32
        )
        for m in range(width // CAP):
            top = m * CAP
            slab = out(m)
            for t in range(5):
                slab[t * CAP : t * CAP + CAP, :] = rows[
                    top : top + CAP, t * 128 : t * 128 + 128
                ].astype(BF)
            slab[80:ROWS, :] = jnp.where(
                half, rows[top : top + 8, 640:768], rows[top + 8 : top + 16, 640:768]
            ).astype(BF)
            post(m)

    def samples_of(slabs):
        columns = [
            jnp.concatenate([slab[t * CAP : t * CAP + CAP, :] for slab in slabs], axis=0)
            for t in range(5)
        ]
        last = []
        for slab in slabs:
            rest = slab[80:ROWS, :].astype(F32)
            last += [jnp.where(half, rest, 0.0), jnp.where(half, 0.0, rest)]
        columns.append(jnp.concatenate(last, axis=0).astype(BF))
        return jnp.concatenate(columns, axis=1)

    def pick_of(first, width):
        lanes = lax.broadcasted_iota(jnp.int32, (512, 128), 1)
        wanted_at = tgt[...]
        return jnp.concatenate(
            [
                jnp.where(wanted_at == lanes + (first + 128 * n), 1.0, 0.0).astype(BF)
                for n in range(width // 128)
            ],
            axis=1,
        )

    def all_of(n, lo):
        part = pl.ds(lo, 16 - lo)
        return pltpu.make_async_remote_copy(
            send.at[n, part], recv.at[n, part], ss.at[n], rs.at[n],
            device_id=(a, b), device_id_type=MESH,
        )

    def place(n):
        @pl.when(n == 0)
        def _():
            all_of(0, 1).wait_recv()

        @pl.when(n > 0)
        def _():
            all_of(n, 0).wait_recv()

        rows = jnp.concatenate(
            [samples_of([recv.at[n, g * 8 + p] for p in range(8)]) for g in range(2)], axis=0
        )
        acc[...] += jnp.dot(pick_of(n * 256, 256), rows, preferred_element_type=F32)

    def step(t, carry):
        n = lax.rem(t + 4, 8)
        @pl.when(n == 0)
        def _():
            own_step().wait_recv()

        @pl.when(n > 0)
        def _():
            requests(n).wait_recv()

        request = [jnp.sum(ask_in[2 * n + g], axis=0, keepdims=True) for g in range(2)]

        def post(m):
            dy, dz = offset(n, m)
            to = lax.rem(y + 4 - dy, 4) * 16 + lax.rem(z + 4 - dz, 4) * 4 + x_down[m % 4]

            def go():
                pltpu.make_async_remote_copy(
                    send.at[n, m],
                    recv.at[n, m],
                    ss.at[n],
                    rs.at[n],
                    device_id=(core[m // 4 % 2], to),
                    device_id_type=MESH,
                ).start()

            if m:
                go()
            else:
                pl.when(n > 0)(go)

        serve(jnp.concatenate(request, axis=1), lambda m: send.at[n, m], post)

        @pl.when(n == 0)
        def _():
            recv[0, 0] = send[0, 0]

        @pl.when(t >= LAG)
        def _():
            place(lax.rem(t + 4 - LAG, 8))

        return carry

    lax.fori_loop(0, 8, step, 0)

    def rest(t, carry):
        place(lax.rem(t + 4, 8))
        return carry

    lax.fori_loop(8 - LAG, 8, rest, 0)

    for n in range(5, 8):
        loads[n].wait()
    lane = lax.broadcasted_iota(jnp.int32, (8, 128), 1)
    node = lax.broadcasted_iota(jnp.int32, (8, 128), 0)
    low = lax.broadcasted_iota(jnp.int32, (128, 128), 1) < 64
    part[...] = jnp.zeros_like(part)

    def store(e):
        return pltpu.make_async_copy(gram.at[e], gram_hbm.at[e], stored.at[e])

    def finish(e, carry):
        here = pl.ds(e * 128, 128)
        w = acc[here, :]
        image = img_ref[here, :].astype(F32)
        tiles = [w[:, n * 128 : n * 128 + 128] for n in range(4)]
        turned = [pltpu.roll(tile, 64, 1) for tile in tiles]
        last = w[:, 640:768]
        turned.append(last + pltpu.roll(last, 64, 1))
        g = [
            jnp.concatenate(
                [jnp.where(low, turned[n], turned[n + 1]) - tiles[n] for n in range(4)], axis=1
            )
        ]
        blocks = [w[:, n * 256 : n * 256 + 256].astype(BF) for n in range(3)]
        halves = [
            jnp.dot(
                jnp.concatenate([blocks[one], blocks[two]], axis=1),
                slope_ref[n],
                preferred_element_type=F32,
            )
            for n, (one, two) in enumerate(BLOCKS)
        ]
        g += [jnp.concatenate(halves[2 * c : 2 * c + 2], axis=1) for c in range(2)]
        r = w[:, :512] - image
        products = jnp.concatenate([(g[c] * g[d]).astype(BF) for c, d in PAIRS], axis=0)
        forces = jnp.concatenate([(g[c] * r).astype(BF) for c in range(3)], axis=1)
        sums = jnp.dot(products, shape_ref[:512, :], preferred_element_type=F32)
        full = []
        for c in range(6):
            by_node = sums[c * 128 : c * 128 + 128, :].T
            full.append(by_node[:64] + by_node[64:])
        force = jnp.dot(forces, shape_ref[512:, :], preferred_element_type=F32).T
        for c in range(3):
            for d in range(3):
                at = PAIRS.index((min(c, d), max(c, d)))
                for n in range(8):
                    row = (c * 8 + n) * 24 + d * 8
                    gram[e, row : row + 8, :] = full[at][n * 8 : n * 8 + 8]
        store(e).start()
        terms = [force[c * 16 : c * 16 + 8] + force[c * 16 + 8 : c * 16 + 16] for c in range(3)]
        for c in range(6):
            diagonal = full[c][0:8]
            for n in range(1, 8):
                diagonal = jnp.where(node == n, full[c][n * 8 : n * 8 + 8], diagonal)
            terms.append(diagonal)
        both = []
        for t in terms:
            moved = jnp.where(lane == 0, 0.0, pltpu.roll(t, 1, 1))
            both.append(t + pltpu.roll(moved, 7, 0))
        for nx in range(2):
            for c in range(9):
                part[nx, e, c : c + 1, :] += both[c][2 * nx : 2 * nx + 1]
                part[nx, e + 1, c : c + 1, :] = both[c][4 + 2 * nx : 5 + 2 * nx]
        return carry

    for e in range(4):
        finish(e, 0)

    right = lax.rem(b + 1, 64)
    to_face = pltpu.make_async_remote_copy(
        part.at[1, pl.ds(0, 4)], face_in, hs.at[0], hr.at[0], device_id=(a, right), device_id_type=MESH
    )
    to_lid = pltpu.make_async_remote_copy(
        part.at[0, 4], lid_in, hs.at[1], hr.at[1], device_id=(1 - a, b), device_id_type=MESH
    )
    to_edge = pltpu.make_async_remote_copy(
        part.at[1, 4], edge_in, hs.at[2], hr.at[2], device_id=(1 - a, right), device_id_type=MESH
    )
    pl.when(b < 63)(to_face.start)
    pl.when(a == 0)(to_lid.start)
    pl.when((a == 0) & (b < 63))(to_edge.start)

    @pl.when(b > 0)
    def _():
        to_face.wait_recv()
        part[0, :4] += face_in[...]

    @pl.when(a == 1)
    def _():
        to_lid.wait_recv()
        part[0, 0] += lid_in[...]

    @pl.when((a == 1) & (b > 0))
    def _():
        to_edge.wait_recv()
        part[0, 0] += edge_in[...]

    for e in range(4):
        for c in range(9):
            nodes[c, e] = part[0, e, c : c + 1, :]
    store_nodes = pltpu.make_async_copy(nodes, nodes_hbm, stored.at[4])
    store_nodes.start()
    pl.when(b < 63)(to_face.wait_send)
    pl.when(a == 0)(to_lid.wait_send)
    pl.when((a == 0) & (b < 63))(to_edge.wait_send)
    own_step().wait_send()
    all_of(0, 1).wait_send()
    for n in range(1, 8):
        requests(n).wait_send()
        all_of(n, 0).wait_send()
    for e in range(4):
        store(e).wait()
    store_nodes.wait()


def copy_kernel(nodes_in, gram_in, nodes_out, gram_out, nodes, gram, came, went):
    moves = [(gram_in.at[e], gram.at[e], gram_out.at[e]) for e in range(4)]
    moves.append((nodes_in, nodes, nodes_out))
    inward = [
        pltpu.make_async_copy(src, mid, came.at[n]) for n, (src, mid, _) in enumerate(moves)
    ]
    outward = [
        pltpu.make_async_copy(mid, dst, went.at[n]) for n, (_, mid, dst) in enumerate(moves)
    ]
    for copy in inward:
        copy.start()
    for before, after in zip(inward, outward):
        before.wait()
        after.start()
    for copy in outward:
        copy.wait()


def run(owner, wanted, classes, bricks, image):
    hbm = pl.BlockSpec(memory_space=pl.ANY)
    dma = pltpu.SemaphoreType.DMA
    ints = pltpu.VMEM((4, 1, 128), jnp.int32)
    outs = (
        jax.ShapeDtypeStruct((9, 4, 1, 128), F32),
        jax.ShapeDtypeStruct((4, 576, 128), F32),
    )
    made = pl.pallas_call(
        kernel,
        out_shape=outs,
        in_specs=[hbm] * 8,
        out_specs=(hbm, hbm),
        scratch_shapes=[
            ints,
            ints,
            ints,
            pltpu.VMEM((4, 1000, 128), BF),
            pltpu.VMEM((4, 320, 128), BF),
            pltpu.VMEM((512, 512), BF),
            pltpu.VMEM((4, 512, 256), BF),
            pltpu.VMEM((2048, 128), BF),
            dma((8,)),
            pltpu.VMEM((16, 8, 128), jnp.int32),
            pltpu.VMEM((16, 8, 128), jnp.int32),
            pltpu.VMEM((512, 128), jnp.int32),
            pltpu.VMEM((800, 2048), BF),
            pltpu.VMEM((768, 256), BF),
            pltpu.VMEM((8, 16, ROWS, 128), BF),
            pltpu.VMEM((8, 16, ROWS, 128), BF),
            pltpu.VMEM((512, 768), F32),
            pltpu.VMEM((4, 576, 128), F32),
            pltpu.VMEM((9, 4, 1, 128), F32),
            pltpu.VMEM((2, 5, 16, 128), F32),
            pltpu.VMEM((4, 16, 128), F32),
            pltpu.VMEM((16, 128), F32),
            pltpu.VMEM((16, 128), F32),
            dma((8,)),
            dma((8,)),
            dma((8,)),
            dma((8,)),
            dma((3,)),
            dma((3,)),
            dma((5,)),
        ],
        compiler_params=pltpu.CompilerParams(
            collective_id=0, has_side_effects=True, vmem_limit_bytes=60 << 20
        ),
    )(
        owner,
        wanted,
        classes,
        bricks,
        jnp.asarray(selection_table()),
        image,
        jnp.asarray(slope_table()),
        jnp.asarray(shape_tables()),
    )
    return pl.pallas_call(
        copy_kernel,
        out_shape=outs,
        in_specs=[hbm] * 2,
        out_specs=(hbm, hbm),
        scratch_shapes=[
            pltpu.VMEM((9, 4, 1, 128), F32),
            pltpu.VMEM((4, 576, 128), F32),
            dma((5,)),
            dma((5,)),
        ],
        compiler_params=pltpu.CompilerParams(vmem_limit_bytes=60 << 20),
    )(*made)


def per_device(image, bricks, owner, brick_index, offset_class):
    bricks = jnp.transpose(bricks.reshape(4, 128, 1000), (0, 2, 1))
    nodes, gram = run(
        owner.reshape(4, 1, 128),
        brick_index.reshape(4, 1, 128),
        offset_class.reshape(4, 1, 128),
        bricks,
        image.reshape(512, 512),
    )
    return (nodes, jnp.transpose(gram, (0, 2, 1)).reshape(1, 1, 4, 1, 128, 576))


def solution(mesh):
    wide = P("gz", "xy", None, None, None, None)
    narrow = P("gz", "xy", None, None, None)
    return jax.shard_map(
        per_device,
        mesh=mesh,
        in_specs=(wide, wide, wide, narrow, narrow),
        out_specs=(P(None, "gz", "xy", None), wide),
        check_vma=False,
    )
```

```python
import jax
import jax.numpy as jnp
import ml_dtypes
import numpy as np
from jax import lax
from jax.experimental import pallas as pl
from jax.experimental.pallas import tpu as pltpu
from jax.sharding import PartitionSpec as P

MESH = pl.DeviceIdType.MESH
CAP = 16
BF = jnp.bfloat16
F32 = jnp.float32
NT = (((1,), (1,)), ((), ()))


def bf16_const(values):
    return np.asarray(values, np.float32).astype(ml_dtypes.bfloat16)


def selection_table():
    where = [(j, k) for j in range(8) for k in range(8)]
    where += [(j, 8) for j in range(8)] + [(8, k) for k in range(8)]
    table = np.zeros((4, 320, 128), np.float32)
    for phase in range(4):
        for shift in range(4):
            for row, (j, k) in enumerate(where):
                src = (j + shift // 2) * 10 + k + shift % 2
                table[phase, shift * 80 + row, phase * 4 + src] = 1.0
    return bf16_const(table)


BLOCKS = ((0, 2), (1, 2), (0, 2), (1, 2))


def slope_table():
    def at(i, j, k):
        if k == 8:
            return 512 + i * 16 + j
        if j == 8:
            return 512 + i * 16 + 8 + k
        return i * 64 + j * 8 + k

    table = np.zeros((768, 1024), np.float32)
    for i in range(8):
        for j in range(8):
            for k in range(8):
                v = at(i, j, k)
                for c, up in enumerate((at(i, j + 1, k), at(i, j, k + 1))):
                    table[up, c * 512 + v] = 1.0
                    table[v, c * 512 + v] = -1.0
    blocks = []
    for n, (one, two) in enumerate(BLOCKS):
        columns = table[:, n * 256 : n * 256 + 256]
        blocks.append(
            np.concatenate([columns[one * 256 : one * 256 + 256], columns[two * 256 : two * 256 + 256]])
        )
    return bf16_const(np.stack(blocks))


def split_rows(rows):
    high = bf16_const(rows)
    low = bf16_const(rows - high.astype(np.float64))
    return np.concatenate([high, low], axis=0)


def shape_tables():
    t = (np.arange(8, dtype=np.float64) + 0.5) / 8.0
    rows = []
    for n in range(8):
        az = t if n // 4 else 1.0 - t
        ax = t if n // 2 % 2 else 1.0 - t
        ay = t if n % 2 else 1.0 - t
        rows.append((az[:, None, None] * ax[None, :, None] * ay[None, None, :]).reshape(512))
    shape = np.stack(rows)
    full = (shape[:, None, :] * shape[None, :, :]).reshape(64, 512) / 64.0
    table = np.zeros((2048, 128), ml_dtypes.bfloat16)
    table[:512] = split_rows(full).T
    for c in range(3):
        table[512 + c * 512 : 1024 + c * 512, c * 16 : c * 16 + 16] = split_rows(shape / 64.0).T
    return table


PAIRS = ((0, 0), (0, 1), (0, 2), (1, 1), (1, 2), (2, 2))
LAG = 4
FARTHEST_FIRST = sorted(
    (
        (-min(dy, 4 - dy) - min(dz, 4 - dz) - min(dx, 4 - dx), da, dy, dz, dx)
        for da in range(2)
        for dy in range(4)
        for dz in range(4)
        for dx in range(4)
        if da or dy or dz or dx
    )
)
ROWS = 88


def kernel(
    own_hbm, idx_hbm, cls_hbm, brick_hbm, sel_hbm, img_hbm, slope_hbm, shape_hbm, nodes_hbm, gram_hbm,
    own_ref, idx_ref, cls_ref, brick_ref, sel_ref, img_ref, slope_ref, shape_ref, loaded,
    earlier, ask_out, ask_in, tgt, lhs, wide, send, recv, acc,
    gram, nodes, part, face_in, lid_in, edge_in,
    asked, asks, ss, rs, hs, hr, stored,
):
    a = lax.axis_index("gz")
    b = lax.axis_index("xy")
    y, z, x = lax.div(b, 16), lax.rem(lax.div(b, 4), 4), lax.rem(b, 4)
    core = [a, 1 - a]
    x_up = [lax.rem(x + d, 4) for d in range(4)]
    y_up = [lax.rem(y + d, 4) for d in range(4)]
    z_up = [lax.rem(z + d, 4) for d in range(4)]
    x_down = [lax.rem(x + 4 - d, 4) for d in range(4)]

    loads = []
    for n, (src, dst) in enumerate(
        (
            (own_hbm, own_ref),
            (idx_hbm, idx_ref),
            (cls_hbm, cls_ref),
            (brick_hbm, brick_ref),
            (sel_hbm, sel_ref),
            (img_hbm, img_ref),
            (slope_hbm, slope_ref),
            (shape_hbm, shape_ref),
        )
    ):
        loads.append(pltpu.make_async_copy(src, dst, loaded.at[n]))
    for n in range(3):
        loads[n].start()
    barrier = pltpu.get_barrier_semaphore()
    for far, da, dy, dz, dx in FARTHEST_FIRST:
        pl.semaphore_signal(
            barrier,
            inc=1,
            device_id=(core[da], y_up[dy] * 16 + z_up[dz] * 4 + x_up[dx]),
            device_id_type=MESH,
        )
    for n in range(3, 5):
        loads[n].start()
    before = (
        lax.broadcasted_iota(jnp.int32, (512, 512), 0)
        < lax.broadcasted_iota(jnp.int32, (512, 512), 1)
    ).astype(F32).astype(BF)
    earlier[...] = before
    for n in range(3):
        loads[n].wait()

    def row_of(ref):
        return jnp.concatenate([ref[i] for i in range(4)], axis=1)

    owner, wanted, classes = row_of(own_ref), row_of(idx_ref), row_of(cls_ref)
    off_core = ((owner >> 6) + a) & 1
    off_y = ((owner >> 4) - y) & 3
    off_z = ((owner >> 2) - z) & 3
    off_x = (owner - x) & 3
    p_of = off_core * 4 + off_x
    jy = (off_y - off_x) & 3
    jz = (off_z - 2 * off_core - off_x) & 3
    message = (jy * 2 + (jz >> 1)) * 16 + (jz & 1) * 8 + p_of
    sub = lax.broadcasted_iota(jnp.int32, (128, 512), 0)
    hit = sub == message
    onehot = hit.astype(F32).astype(BF)
    ahead = jnp.dot(onehot, earlier[...], preferred_element_type=F32)
    slot = jnp.sum(jnp.where(hit, ahead, 0.0), axis=0, keepdims=True).astype(jnp.int32)
    target = message * CAP + slot
    tgt[...] = jnp.broadcast_to(target, (128, 512)).T
    in_slot = (sub & 15) == slot
    low = jnp.where(in_slot, wanted & 255, 0).astype(F32).astype(BF)
    high = jnp.where(in_slot, (wanted >> 8) + 2 * classes, 0).astype(F32).astype(BF)
    table = lax.dot_general(
        onehot, jnp.concatenate([low, high], axis=0), NT, preferred_element_type=F32
    )
    table = (table[:, :128] + 256.0 * table[:, 128:]).astype(jnp.int32)
    group = lax.broadcasted_iota(jnp.int32, (128, 128), 0) & 7
    lane = lax.broadcasted_iota(jnp.int32, (128, 128), 1)
    ask_out[...] = jnp.where((lane >> 4) == group, table, 0).reshape(16, 8, 128)

    def offset(n, m):
        dy = lax.rem(lax.div(n, 2) + m % 4, 4)
        dz = lax.rem(2 * lax.rem(n, 2) + m // 8 + 2 * (m // 4 % 2) + m % 4, 4)
        return dy, dz

    def ask(n):
        for m in range(16):
            dy, dz = offset(n, m)
            to = lax.rem(y + dy, 4) * 16 + lax.rem(z + dz, 4) * 4 + x_up[m % 4]

            def go(m=m, to=to):
                at = (2 * n + m // 8, pl.ds(m % 8, 1))
                pltpu.make_async_remote_copy(
                    ask_out.at[at],
                    ask_in.at[at],
                    asked.at[n],
                    asks.at[n],
                    device_id=(core[m // 4 % 2], to),
                    device_id_type=MESH,
                ).start()

            if m:
                go()
            elif not isinstance(n, int):
                pl.when(n > 0)(go)
            elif n:
                go()

    def ask_step(t, carry):
        ask(lax.rem(t, 8))
        return carry

    def requests(n):
        at = (pl.ds(2 * n, 2),)
        return pltpu.make_async_remote_copy(
            ask_out.at[at], ask_in.at[at], asked.at[n], asks.at[n],
            device_id=(a, b), device_id_type=MESH,
        )

    def own_step():
        at = (pl.ds(0, 15), pl.ds(0, 1))
        return pltpu.make_async_remote_copy(
            ask_out.at[at], ask_in.at[at], asked.at[0], asks.at[0],
            device_id=(a, b), device_id_type=MESH,
        )

    ask_in[0, 0:1] = ask_out[0, 0:1]
    pl.semaphore_wait(barrier, 127)
    lax.fori_loop(4, 7, ask_step, 0)
    loads[3].wait()
    loads[4].wait()
    for i in range(10):
        start = 100 * i // 16 * 16
        depth = min(112, 1000 - start)
        window = jnp.concatenate([brick_ref[e, start : start + depth, :] for e in range(4)], axis=1)
        picked = jnp.dot(
            sel_ref[100 * i % 16 // 4, :, :depth], window, preferred_element_type=F32
        ).astype(BF)
        for shift in range(4):
            lhs[i * 80 : i * 80 + 80, shift * 512 : shift * 512 + 512] = picked[
                shift * 80 : shift * 80 + 80
            ]

    lax.fori_loop(7, 12, ask_step, 0)
    for n in range(5, 8):
        loads[n].start()

    acc[...] = jnp.zeros_like(acc)

    eye = (
        lax.broadcasted_iota(jnp.int32, (256, 256), 0)
        == lax.broadcasted_iota(jnp.int32, (256, 256), 1)
    ).astype(F32).astype(BF)
    half = lax.broadcasted_iota(jnp.int32, (8, 128), 1) < 64

    def serve(request, out, post):
        width = request.shape[1]
        brick = request & 511
        cls = request >> 9
        fz = ((cls >> 4).astype(F32) + 0.5) * 0.25
        fx = (((cls >> 2) & 3).astype(F32) + 0.5) * 0.25
        fy = ((cls & 3).astype(F32) + 0.5) * 0.25
        match = lax.broadcasted_iota(jnp.int32, (512, width), 0) == brick
        weights = []
        for shift in range(4):
            wx = fx if shift // 2 else 1.0 - fx
            wy = fy if shift % 2 else 1.0 - fy
            weights.append(jnp.where(match, wx * wy, 0.0).astype(BF))
        layers = jnp.dot(lhs[...], jnp.concatenate(weights, axis=0), preferred_element_type=F32)
        for i in range(9):
            here = layers[i * 80 : i * 80 + 80] * (1.0 - fz)
            here = here + layers[i * 80 + 80 : i * 80 + 160] * fz
            here = here.astype(BF)
            if i < 8:
                wide[i * 64 : i * 64 + 64, :width] = here[:64]
                wide[512 + i * 16 : 528 + i * 16, :width] = here[64:]
            else:
                wide[640:704, :width] = here[:64]
                wide[704:768, :width] = here[:64]
        rows = lax.dot_general(
            eye[:width, :width], wide[:, :width], NT, preferred_element_type=F32
        )
        for m in range(width // CAP):
            top = m * CAP
            slab = out(m)
            for t in range(5):
                slab[t * CAP : t * CAP + CAP, :] = rows[
                    top : top + CAP, t * 128 : t * 128 + 128
                ].astype(BF)
            slab[80:ROWS, :] = jnp.where(
                half, rows[top : top + 8, 640:768], rows[top + 8 : top + 16, 640:768]
            ).astype(BF)
            post(m)

    def samples_of(slabs):
        columns = [
            jnp.concatenate([slab[t * CAP : t * CAP + CAP, :] for slab in slabs], axis=0)
            for t in range(5)
        ]
        last = []
        for slab in slabs:
            rest = slab[80:ROWS, :].astype(F32)
            last += [jnp.where(half, rest, 0.0), jnp.where(half, 0.0, rest)]
        columns.append(jnp.concatenate(last, axis=0).astype(BF))
        return jnp.concatenate(columns, axis=1)

    def pick_of(first, width):
        lanes = lax.broadcasted_iota(jnp.int32, (512, 128), 1)
        wanted_at = tgt[...]
        return jnp.concatenate(
            [
                jnp.where(wanted_at == lanes + (first + 128 * n), 1.0, 0.0).astype(BF)
                for n in range(width // 128)
            ],
            axis=1,
        )

    def all_of(n, lo):
        part = pl.ds(lo, 16 - lo)
        return pltpu.make_async_remote_copy(
            send.at[n, part], recv.at[n, part], ss.at[n], rs.at[n],
            device_id=(a, b), device_id_type=MESH,
        )

    def place(n):
        @pl.when(n == 0)
        def _():
            all_of(0, 1).wait_recv()

        @pl.when(n > 0)
        def _():
            all_of(n, 0).wait_recv()

        rows = jnp.concatenate(
            [samples_of([recv.at[n, g * 8 + p] for p in range(8)]) for g in range(2)], axis=0
        )
        acc[...] += jnp.dot(pick_of(n * 256, 256), rows, preferred_element_type=F32)

    def step(t, carry):
        n = lax.rem(t + 4, 8)
        @pl.when(n == 0)
        def _():
            own_step().wait_recv()

        @pl.when(n > 0)
        def _():
            requests(n).wait_recv()

        request = [jnp.sum(ask_in[2 * n + g], axis=0, keepdims=True) for g in range(2)]

        def post(m):
            dy, dz = offset(n, m)
            to = lax.rem(y + 4 - dy, 4) * 16 + lax.rem(z + 4 - dz, 4) * 4 + x_down[m % 4]

            def go():
                pltpu.make_async_remote_copy(
                    send.at[n, m],
                    recv.at[n, m],
                    ss.at[n],
                    rs.at[n],
                    device_id=(core[m // 4 % 2], to),
                    device_id_type=MESH,
                ).start()

            if m:
                go()
            else:
                pl.when(n > 0)(go)

        serve(jnp.concatenate(request, axis=1), lambda m: send.at[n, m], post)

        @pl.when(n == 0)
        def _():
            recv[0, 0] = send[0, 0]

        @pl.when(t >= LAG)
        def _():
            place(lax.rem(t + 4 - LAG, 8))

        return carry

    lax.fori_loop(0, 8, step, 0)

    def rest(t, carry):
        place(lax.rem(t + 4, 8))
        return carry

    lax.fori_loop(8 - LAG, 8, rest, 0)

    for n in range(5, 8):
        loads[n].wait()
    lane = lax.broadcasted_iota(jnp.int32, (8, 128), 1)
    node = lax.broadcasted_iota(jnp.int32, (8, 128), 0)
    low = lax.broadcasted_iota(jnp.int32, (128, 128), 1) < 64
    part[...] = jnp.zeros_like(part)

    def store(e):
        return pltpu.make_async_copy(gram.at[e], gram_hbm.at[e], stored.at[e])

    fulls = []

    def finish(e, carry):
        here = pl.ds(e * 128, 128)
        w = acc[here, :]
        image = img_ref[here, :].astype(F32)
        tiles = [w[:, n * 128 : n * 128 + 128] for n in range(4)]
        turned = [pltpu.roll(tile, 64, 1) for tile in tiles]
        last = w[:, 640:768]
        turned.append(last + pltpu.roll(last, 64, 1))
        g = [
            jnp.concatenate(
                [jnp.where(low, turned[n], turned[n + 1]) - tiles[n] for n in range(4)], axis=1
            )
        ]
        blocks = [w[:, n * 256 : n * 256 + 256].astype(BF) for n in range(3)]
        halves = [
            jnp.dot(
                jnp.concatenate([blocks[one], blocks[two]], axis=1),
                slope_ref[n],
                preferred_element_type=F32,
            )
            for n, (one, two) in enumerate(BLOCKS)
        ]
        g += [jnp.concatenate(halves[2 * c : 2 * c + 2], axis=1) for c in range(2)]
        r = w[:, :512] - image
        products = jnp.concatenate([(g[c] * g[d]).astype(BF) for c, d in PAIRS], axis=0)
        forces = jnp.concatenate([(g[c] * r).astype(BF) for c in range(3)], axis=1)
        sums = jnp.dot(products, shape_ref[:512, :], preferred_element_type=F32)
        full = []
        for c in range(6):
            by_node = sums[c * 128 : c * 128 + 128, :].T
            full.append(by_node[:64] + by_node[64:])
        force = jnp.dot(forces, shape_ref[512:, :], preferred_element_type=F32).T
        fulls.append(full)
        terms = [force[c * 16 : c * 16 + 8] + force[c * 16 + 8 : c * 16 + 16] for c in range(3)]
        for c in range(6):
            diagonal = full[c][0:8]
            for n in range(1, 8):
                diagonal = jnp.where(node == n, full[c][n * 8 : n * 8 + 8], diagonal)
            terms.append(diagonal)
        both = []
        for t in terms:
            moved = jnp.where(lane == 0, 0.0, pltpu.roll(t, 1, 1))
            both.append(t + pltpu.roll(moved, 7, 0))
        for nx in range(2):
            for c in range(9):
                part[nx, e, c : c + 1, :] += both[c][2 * nx : 2 * nx + 1]
                part[nx, e + 1, c : c + 1, :] = both[c][4 + 2 * nx : 5 + 2 * nx]
        return carry

    for e in range(4):
        finish(e, 0)

    right = lax.rem(b + 1, 64)
    to_face = pltpu.make_async_remote_copy(
        part.at[1, pl.ds(0, 4)], face_in, hs.at[0], hr.at[0], device_id=(a, right), device_id_type=MESH
    )
    to_lid = pltpu.make_async_remote_copy(
        part.at[0, 4], lid_in, hs.at[1], hr.at[1], device_id=(1 - a, b), device_id_type=MESH
    )
    to_edge = pltpu.make_async_remote_copy(
        part.at[1, 4], edge_in, hs.at[2], hr.at[2], device_id=(1 - a, right), device_id_type=MESH
    )
    pl.when(b < 63)(to_face.start)
    pl.when(a == 0)(to_lid.start)
    pl.when((a == 0) & (b < 63))(to_edge.start)

    for e in range(4):
        for c in range(3):
            for d in range(3):
                at = PAIRS.index((min(c, d), max(c, d)))
                for n in range(8):
                    row = (c * 8 + n) * 24 + d * 8
                    gram[e, row : row + 8, :] = fulls[e][at][n * 8 : n * 8 + 8]
        store(e).start()

    @pl.when(b > 0)
    def _():
        to_face.wait_recv()
        part[0, :4] += face_in[...]

    @pl.when(a == 1)
    def _():
        to_lid.wait_recv()
        part[0, 0] += lid_in[...]

    @pl.when((a == 1) & (b > 0))
    def _():
        to_edge.wait_recv()
        part[0, 0] += edge_in[...]

    for e in range(4):
        for c in range(9):
            nodes[c, e] = part[0, e, c : c + 1, :]
    store_nodes = pltpu.make_async_copy(nodes, nodes_hbm, stored.at[4])
    store_nodes.start()
    pl.when(b < 63)(to_face.wait_send)
    pl.when(a == 0)(to_lid.wait_send)
    pl.when((a == 0) & (b < 63))(to_edge.wait_send)
    own_step().wait_send()
    all_of(0, 1).wait_send()
    for n in range(1, 8):
        requests(n).wait_send()
        all_of(n, 0).wait_send()
    for e in range(4):
        store(e).wait()
    store_nodes.wait()


def copy_kernel(nodes_in, gram_in, nodes_out, gram_out, nodes, gram, came, went):
    moves = [(gram_in.at[e], gram.at[e], gram_out.at[e]) for e in range(4)]
    moves.append((nodes_in, nodes, nodes_out))
    inward = [
        pltpu.make_async_copy(src, mid, came.at[n]) for n, (src, mid, _) in enumerate(moves)
    ]
    outward = [
        pltpu.make_async_copy(mid, dst, went.at[n]) for n, (_, mid, dst) in enumerate(moves)
    ]
    for copy in inward:
        copy.start()
    for before, after in zip(inward, outward):
        before.wait()
        after.start()
    for copy in outward:
        copy.wait()


def run(owner, wanted, classes, bricks, image):
    hbm = pl.BlockSpec(memory_space=pl.ANY)
    dma = pltpu.SemaphoreType.DMA
    ints = pltpu.VMEM((4, 1, 128), jnp.int32)
    outs = (
        jax.ShapeDtypeStruct((9, 4, 1, 128), F32),
        jax.ShapeDtypeStruct((4, 576, 128), F32),
    )
    made = pl.pallas_call(
        kernel,
        out_shape=outs,
        in_specs=[hbm] * 8,
        out_specs=(hbm, hbm),
        scratch_shapes=[
            ints,
            ints,
            ints,
            pltpu.VMEM((4, 1000, 128), BF),
            pltpu.VMEM((4, 320, 128), BF),
            pltpu.VMEM((512, 512), BF),
            pltpu.VMEM((4, 512, 256), BF),
            pltpu.VMEM((2048, 128), BF),
            dma((8,)),
            pltpu.VMEM((512, 512), BF),
            pltpu.VMEM((16, 8, 128), jnp.int32),
            pltpu.VMEM((16, 8, 128), jnp.int32),
            pltpu.VMEM((512, 128), jnp.int32),
            pltpu.VMEM((800, 2048), BF),
            pltpu.VMEM((768, 256), BF),
            pltpu.VMEM((8, 16, ROWS, 128), BF),
            pltpu.VMEM((8, 16, ROWS, 128), BF),
            pltpu.VMEM((512, 768), F32),
            pltpu.VMEM((4, 576, 128), F32),
            pltpu.VMEM((9, 4, 1, 128), F32),
            pltpu.VMEM((2, 5, 16, 128), F32),
            pltpu.VMEM((4, 16, 128), F32),
            pltpu.VMEM((16, 128), F32),
            pltpu.VMEM((16, 128), F32),
            dma((8,)),
            dma((8,)),
            dma((8,)),
            dma((8,)),
            dma((3,)),
            dma((3,)),
            dma((5,)),
        ],
        compiler_params=pltpu.CompilerParams(
            collective_id=0, has_side_effects=True, vmem_limit_bytes=60 << 20
        ),
    )(
        owner,
        wanted,
        classes,
        bricks,
        jnp.asarray(selection_table()),
        image,
        jnp.asarray(slope_table()),
        jnp.asarray(shape_tables()),
    )
    return pl.pallas_call(
        copy_kernel,
        out_shape=outs,
        in_specs=[hbm] * 2,
        out_specs=(hbm, hbm),
        scratch_shapes=[
            pltpu.VMEM((9, 4, 1, 128), F32),
            pltpu.VMEM((4, 576, 128), F32),
            dma((5,)),
            dma((5,)),
        ],
        compiler_params=pltpu.CompilerParams(vmem_limit_bytes=60 << 20),
    )(*made)


def per_device(image, bricks, owner, brick_index, offset_class):
    bricks = jnp.transpose(bricks.reshape(4, 128, 1000), (0, 2, 1))
    nodes, gram = run(
        owner.reshape(4, 1, 128),
        brick_index.reshape(4, 1, 128),
        offset_class.reshape(4, 1, 128),
        bricks,
        image.reshape(512, 512),
    )
    return (nodes, jnp.transpose(gram, (0, 2, 1)).reshape(1, 1, 4, 1, 128, 576))


def solution(mesh):
    wide = P("gz", "xy", None, None, None, None)
    narrow = P("gz", "xy", None, None, None)
    return jax.shard_map(
        per_device,
        mesh=mesh,
        in_specs=(wide, wide, wide, narrow, narrow),
        out_specs=(P(None, "gz", "xy", None), wide),
        check_vma=False,
    )
```
